32 devices in a mesh: dp: 16 (over z, y, x), pipe: 2 (over core).
Axes of the slice: x: 2, y: 2, z: 4, core: 2. Of those that a mesh axis runs over, the one named last changes fastest.
Arguments:
- hidden_in: bfloat16 [4096, 2048], P(('dp', 'pipe')), may hold values from -6 to 6
- grad_out: bfloat16 [4096, 2048], P(('dp', 'pipe')), may hold values from -1.1953125 to 1.1953125
- w_query: bfloat16 [2, 2048, 512], P('pipe'), may hold values from -0.125 to 0.125
- w_key: bfloat16 [2, 2048, 512], P('pipe'), may hold values from -0.125 to 0.125
- w_value: bfloat16 [2, 2048, 512], P('pipe'), may hold values from -0.125 to 0.125
- w_out: bfloat16 [2, 512, 2048], P('pipe'), may hold values from -0.1875 to 0.1875
- pattern: int32 [4, 3], replicated, may hold values from 0 to 3, as said below
Outputs:
- hidden_out: bfloat16 [4096, 2048], P(('dp', 'pipe'))
- grad_in: bfloat16 [4096, 2048], P(('dp', 'pipe'))
- grad_query: float32 [2, 2048, 512], P('pipe', 'dp')
- grad_key: float32 [2, 2048, 512], P('pipe', 'dp')
- grad_value: float32 [2, 2048, 512], P('pipe', 'dp')
- grad_wout: float32 [2, 512, 2048], P('pipe', 'dp')
The draws below stay inside these ranges and needn't reach their ends.
Inputs may be any that keep to these rules, and one draw needn't show every extreme that they name: `pattern`: row i lists key blocks for query block i: entry 0 is i, entry 1 is the block before i (i itself for the first block), the others are blocks no later than i; a row may repeat an entry.
All inputs are finite; a program needn't handle non-finite values.
Results may differ from the reference program's by a relative error of at most 0.023.
Values may be sent and summed in bfloat16 or wider, within the bound.
No kernel may reach another device: no remote copies, remote signals or barrier semaphores. Data moves between devices by JAX's collectives and lax.ppermute only.
A program may use at most 128 MiB of HBM per device.

```python
import math
import jax
import jax.numpy as jnp
from jax import lax

D = 2048
HEADS = 16
HDIM = 64
BLK = 32
KSEL = 3
SEQ = 128
HALF = 512
QB = 4
SLOTS = 2
REPLICAS = 16
ROWS = 4096


def draw_pattern(key, part):
    row_ids = jnp.arange(QB, dtype=jnp.int32)[:, None]
    raw_ints = jax.random.randint(key, (QB, KSEL), 0, 1048576, dtype=jnp.int32)
    picked = raw_ints % (row_ids + 1)
    slot_ids = jnp.arange(KSEL, dtype=jnp.int32)[None, :]
    previous = jnp.maximum(row_ids - 1, 0)
    return jnp.where(slot_ids == 0, row_ids, jnp.where(slot_ids == 1, previous, picked)).astype(jnp.int32)


def strengthened(values, own_key, source, target, parts, factor):
    def block_of(dim):
        return (jnp.arange(values.shape[dim]) // (values.shape[dim] // parts)).reshape((-1,) + (1,) * (values.ndim - 1 - dim))

    first = jax.random.permutation(own_key, parts)[block_of(target)]
    other_side = (block_of(target) + parts // 2) % parts
    return jnp.where((block_of(source) == first) | (block_of(source) == other_side), factor * values, values)


def shard_levels(own_key, shape, pieces, smallest, high):
    def one(axis_at, shards_of):
        draws = jax.random.uniform(jax.random.fold_in(jax.random.fold_in(own_key, 6), axis_at), (shards_of,), jnp.float32, smallest / len(pieces), high / len(pieces))
        return jnp.repeat(jnp.exp(draws), shape[axis_at] // shards_of).reshape((-1,) + (1,) * (len(shape) - axis_at - 1))

    loudness = one(*pieces[0])
    for cut in pieces[1:]:
        loudness = loudness * one(*cut)
    return loudness


def centred(rng, shape, deviation, bound, split=(), kind=jnp.bfloat16):
    entries = deviation * jax.random.normal(rng, shape, jnp.float32)
    if split:
        entries = entries * shard_levels(rng, shape, split, -0.22, 0.18)
    return jnp.clip(entries, -bound, bound).astype(kind)


def heavy_noise(key, extent, spread, reach, shards, heavy, kind=jnp.bfloat16):
    array = spread * jax.random.normal(key, extent, jnp.float32)
    if shards:
        array = array * shard_levels(key, extent, shards, -0.22, 0.18)
    return jnp.clip(strengthened(array, jax.random.fold_in(key, 3), *heavy), -reach, reach).astype(kind)


def setup_inputs(seed: int = 0) -> dict:
    seeds = jax.random.split(jax.random.key(seed), 8)
    hidden_in = heavy_noise(seeds[0], (ROWS, D), 1.0, 6.0, ((0, 32),), (0, 1, 32, 2.75))
    grad_out = centred(seeds[1], (ROWS, D), 0.2, 1.1953125, ((0, 32),))
    w_query = centred(seeds[2], (SLOTS, D, HALF), D ** -0.5, 0.125, ((0, 2),))
    w_key = centred(seeds[3], (SLOTS, D, HALF), D ** -0.5, 0.125, ((0, 2),))
    w_value = centred(seeds[4], (SLOTS, D, HALF), D ** -0.5, 0.125, ((0, 2),))
    w_out = centred(seeds[5], (SLOTS, HALF, D), (HEADS * HDIM) ** -0.5, 0.1875, ((0, 2),))
    pattern = draw_pattern(jax.random.fold_in(seeds[7], 71), 0)
    return dict(hidden_in=hidden_in, grad_out=grad_out, w_query=w_query, w_key=w_key, w_value=w_value, w_out=w_out, pattern=pattern)


NORM_EPS = 1e-05

def visible_mask(pattern, block_len):
    blocks, slot_count = pattern.shape
    equal_slot = pattern[:, :, None] == pattern[:, None, :]
    before = jnp.arange(slot_count)[None, :] < jnp.arange(slot_count)[:, None]
    repeated = jnp.any(equal_slot & before[None, :, :], axis=2)
    row_ids = jnp.arange(block_len)[:, None]
    column_ids = jnp.arange(block_len)[None, :]
    diagonal = pattern == jnp.arange(blocks, dtype=jnp.int32)[:, None]
    allowed = jnp.where(diagonal[:, :, None, None], (column_ids <= row_ids)[None, None], True)
    visible = allowed & jnp.logical_not(repeated)[:, :, None, None]
    return jnp.transpose(visible, (0, 2, 1, 3))

def contract(left_factor, right_factor):
    return lax.dot_general(left_factor, right_factor, (((0,), (0,)), ((), ())), preferred_element_type=jnp.float32)

def replica_sum(left_factor, right_factor):
    left_split = left_factor.reshape(2, REPLICAS, SEQ, left_factor.shape[1])
    right_split = right_factor.reshape(2, REPLICAS, SEQ, right_factor.shape[1])

    def add_replica(total, index):
        left_piece = lax.dynamic_index_in_dim(left_split, index, 1, keepdims=False).reshape(2 * SEQ, left_factor.shape[1])
        right_piece = lax.dynamic_index_in_dim(right_split, index, 1, keepdims=False).reshape(2 * SEQ, right_factor.shape[1])
        rounded = lax.optimization_barrier(contract(left_piece, right_piece).astype(jnp.bfloat16))
        return (total + rounded.astype(jnp.float32), None)
    start = jnp.zeros((left_factor.shape[1], right_factor.shape[1]), jnp.float32)
    total, unused = lax.scan(add_replica, start, jnp.arange(REPLICAS, dtype=jnp.int32))
    return total

def attend_forward(inputs, query_w, key_w, value_w, out_w, pattern, head_dim, block_len):
    amount, seq_len, features = inputs.shape
    blocks = seq_len // block_len
    head_count = query_w.shape[1] // head_dim
    input_f32 = inputs.astype(jnp.float32)
    factor = lax.rsqrt(lax.optimization_barrier(jnp.mean(input_f32 * input_f32, axis=-1, keepdims=True)) + NORM_EPS)
    normed = (input_f32 * factor).astype(jnp.bfloat16).reshape(amount * seq_len, features)
    query = jnp.dot(normed, query_w, preferred_element_type=jnp.float32).astype(jnp.bfloat16)
    key_proj = jnp.dot(normed, key_w, preferred_element_type=jnp.float32).astype(jnp.bfloat16)
    values = jnp.dot(normed, value_w, preferred_element_type=jnp.float32).astype(jnp.bfloat16)
    blocked = (amount, blocks, block_len, head_count, head_dim)
    query_blocks = query.reshape(blocked)
    keys_seen = jnp.take(key_proj.reshape(blocked), pattern, axis=1)
    values_seen = jnp.take(values.reshape(blocked), pattern, axis=1)
    inv_sqrt = 1.0 / math.sqrt(head_dim)
    scores = jnp.einsum('mqihd,mqsjhd->mqhisj', query_blocks.astype(jnp.float32), keys_seen.astype(jnp.float32)) * inv_sqrt
    visible = visible_mask(pattern, block_len)[None, :, None]
    expo = jnp.where(visible, jnp.exp(scores), 0.0)
    totals = lax.optimization_barrier(jnp.sum(expo, axis=(4, 5), keepdims=True))
    prob_f32 = expo / totals
    prob_bf16 = prob_f32.astype(jnp.bfloat16)
    attended = jnp.einsum('mqhisj,mqsjhd->mqihd', prob_bf16.astype(jnp.float32), values_seen.astype(jnp.float32))
    attended = attended.astype(jnp.bfloat16).reshape(amount * seq_len, head_count * head_dim)
    contrib = jnp.dot(attended, out_w, preferred_element_type=jnp.float32).astype(jnp.bfloat16)
    stash_fwd = (input_f32, factor, normed, query_blocks, keys_seen, values_seen, prob_f32, prob_bf16, attended)
    return (contrib.reshape(amount, seq_len, features), stash_fwd)

def attend_backward(stash_fwd, cotangent, query_w, key_w, value_w, out_w, pattern, head_dim, block_len):
    input_f32, factor, normed, query_blocks, keys_seen, values_seen, prob_f32, prob_bf16, attended = stash_fwd
    amount, seq_len, features = cotangent.shape
    blocks = seq_len // block_len
    head_count = query_w.shape[1] // head_dim
    inv_sqrt = 1.0 / math.sqrt(head_dim)
    grad_flat = cotangent.reshape(amount * seq_len, features)
    grad_attended = lax.dot_general(grad_flat, out_w, (((1,), (1,)), ((), ())), preferred_element_type=jnp.float32)
    grad_attended = grad_attended.astype(jnp.bfloat16).reshape(amount, blocks, block_len, head_count, head_dim)
    grad_prob = jnp.einsum('mqihd,mqsjhd->mqhisj', grad_attended.astype(jnp.float32), values_seen.astype(jnp.float32))
    grad_valseen = jnp.einsum('mqhisj,mqihd->mqsjhd', prob_bf16.astype(jnp.float32), grad_attended.astype(jnp.float32))
    inner_sum = lax.optimization_barrier(jnp.sum(prob_f32 * grad_prob, axis=(4, 5), keepdims=True))
    grad_score = (prob_f32 * (grad_prob - inner_sum) * inv_sqrt).astype(jnp.bfloat16)
    grad_querypos = jnp.einsum('mqhisj,mqsjhd->mqihd', grad_score.astype(jnp.float32), keys_seen.astype(jnp.float32))
    grad_querypos = grad_querypos.astype(jnp.bfloat16).reshape(amount * seq_len, head_count * head_dim)
    grad_keyseen = jnp.einsum('mqhisj,mqihd->mqsjhd', grad_score.astype(jnp.float32), query_blocks.astype(jnp.float32))
    onehot = (pattern[:, :, None] == jnp.arange(blocks, dtype=jnp.int32)[None, None, :]).astype(jnp.float32)
    grad_keypos = jnp.einsum('qsk,mqsjhd->mkjhd', onehot, grad_keyseen, precision=lax.Precision.HIGHEST)
    grad_keypos = grad_keypos.astype(jnp.bfloat16).reshape(amount * seq_len, head_count * head_dim)
    grad_valuepos = jnp.einsum('qsk,mqsjhd->mkjhd', onehot, grad_valseen, precision=lax.Precision.HIGHEST)
    grad_valuepos = grad_valuepos.astype(jnp.bfloat16).reshape(amount * seq_len, head_count * head_dim)
    dims = (((1,), (1,)), ((), ()))
    grad_normed = lax.dot_general(grad_querypos, query_w, dims, preferred_element_type=jnp.float32)
    grad_normed = grad_normed + lax.dot_general(grad_keypos, key_w, dims, preferred_element_type=jnp.float32)
    grad_normed = grad_normed + lax.dot_general(grad_valuepos, value_w, dims, preferred_element_type=jnp.float32)
    grad_normed = grad_normed.reshape(amount, seq_len, features)
    mean_term = lax.optimization_barrier(jnp.mean(input_f32 * grad_normed, axis=-1, keepdims=True))
    returned = (factor * grad_normed - input_f32 * factor * factor * factor * mean_term).astype(jnp.bfloat16)
    factor_pairs = ((normed, grad_querypos), (normed, grad_keypos), (normed, grad_valuepos), (attended, grad_flat))
    return (returned, factor_pairs)

def reference(hidden_in, grad_out, w_query, w_key, w_value, w_out, pattern):
    sequences = hidden_in.reshape(REPLICAS, SLOTS, SEQ, D)
    cotangents = grad_out.reshape(REPLICAS, SLOTS, SEQ, D)
    outputs = [None] * SLOTS
    input_grads = [None] * SLOTS
    grads = [[None] * SLOTS for position in range(4)]
    for section_idx in range(SLOTS // 2):
        slot_pair = (section_idx, SLOTS - 1 - section_idx)
        inputs = jnp.concatenate([sequences[:, slot_pair[0]], sequences[:, slot_pair[1]]], axis=0)
        cotangent = jnp.concatenate([cotangents[:, slot_pair[0]], cotangents[:, slot_pair[1]]], axis=0)
        summed_out = inputs.astype(jnp.float32)
        summed_in = cotangent.astype(jnp.float32)
        for slot_idx in slot_pair:
            contrib, stash_fwd = attend_forward(inputs, w_query[slot_idx], w_key[slot_idx], w_value[slot_idx], w_out[slot_idx], pattern, HDIM, BLK)
            returned, factor_pairs = attend_backward(stash_fwd, cotangent, w_query[slot_idx], w_key[slot_idx], w_value[slot_idx], w_out[slot_idx], pattern, HDIM, BLK)
            summed_out = summed_out + contrib.astype(jnp.float32)
            summed_in = summed_in + returned.astype(jnp.float32)
            for position in range(4):
                grads[position][slot_idx] = replica_sum(factor_pairs[position][0], factor_pairs[position][1])
        summed_out = summed_out.astype(jnp.bfloat16)
        summed_in = summed_in.astype(jnp.bfloat16)
        outputs[slot_pair[0]] = summed_out[:REPLICAS]
        outputs[slot_pair[1]] = summed_out[REPLICAS:]
        input_grads[slot_pair[0]] = summed_in[:REPLICAS]
        input_grads[slot_pair[1]] = summed_in[REPLICAS:]
    hidden_out = jnp.stack(outputs, axis=1).reshape(ROWS, D)
    grad_in = jnp.stack(input_grads, axis=1).reshape(ROWS, D)
    return (hidden_out, grad_in, jnp.stack(grads[0]), jnp.stack(grads[1]), jnp.stack(grads[2]), jnp.stack(grads[3]))
```

```python
import functools
import math

import jax
import jax.numpy as jnp
from jax import lax
from jax.experimental import pallas as pl
from jax.experimental.pallas import tpu as pltpu
from jax.sharding import PartitionSpec as P

HDIM = 64
NORM_EPS = 1e-05
PAIR = 2 * HDIM
VMEM_BYTES = 40 * 1024 * 1024

F32 = jnp.float32
BF16 = jnp.bfloat16
NT = (((1,), (1,)), ((), ()))
TN = (((0,), (0,)), ((), ()))

ROW_BIT = 0
COL_BIT = 2


def dot(left, right):
    return jnp.dot(left, right, preferred_element_type=F32)


def dot_nt(left, right):
    return lax.dot_general(left, right, NT, preferred_element_type=F32)


def dot_tn(left, right):
    return lax.dot_general(left, right, TN, preferred_element_type=F32)


def call(body, name, inputs, outs, scratch=(), flops=0, scalars=1):
    specs = [pl.BlockSpec(memory_space=pltpu.SMEM)] * scalars
    specs += [pl.BlockSpec(memory_space=pltpu.VMEM)] * (len(inputs) - scalars)
    moved = sum(x.size * x.dtype.itemsize for x in inputs)
    moved += sum(x.size * x.dtype.itemsize for x in outs)
    return pl.pallas_call(
        body,
        name=name,
        out_shape=outs,
        in_specs=specs,
        out_specs=[pl.BlockSpec(memory_space=pltpu.VMEM)] * len(outs),
        scratch_shapes=list(scratch),
        compiler_params=pltpu.CompilerParams(vmem_limit_bytes=VMEM_BYTES),
        cost_estimate=pl.CostEstimate(flops=flops, bytes_accessed=moved, transcendentals=0),
    )(*inputs)


def row_chunks(bit_count, halved_bits):
    order = list(halved_bits) + [COL_BIT]
    chunks = []
    for index in range(1 << len(order)):
        chunk = 0
        for place, bit in enumerate(reversed(order)):
            chunk |= ((index >> place) & 1) << bit
        chunks.append(chunk)
    return chunks


def copy_chunks(source, target, chunks, size, row_bit):
    for place, chunk in enumerate(chunks):
        start = pl.multiple_of((chunk + (row_bit << ROW_BIT)) * size, size)
        target[place * size : (place + 1) * size, :] = source[pl.ds(start, size), :]


def prep_body(chunks, bits, hidden, grad, x_keep, x_send, g_keep, g_send, turned):
    row_bit, col_bit = bits[0], bits[1]
    size = hidden.shape[1] // (2 * len(chunks))
    width = hidden.shape[1] // 2
    turned[...] = hidden[...].astype(F32).T.astype(BF16)
    copy_chunks(turned, x_keep, chunks, size, row_bit)
    copy_chunks(turned, x_send, chunks, size, 1 - row_bit)
    g_keep[...] = grad[:, pl.ds(pl.multiple_of(col_bit * width, width), width)]
    g_send[...] = grad[:, pl.ds(pl.multiple_of((1 - col_bit) * width, width), width)]


def seen_mask(pattern, seq_len, blocks, slots):
    block_len = seq_len // blocks
    rows = lax.broadcasted_iota(jnp.int32, (seq_len, seq_len), 0)
    columns = lax.broadcasted_iota(jnp.int32, (seq_len, seq_len), 1)
    row_block, column_block = rows // block_len, columns // block_len
    seen = jnp.zeros((seq_len, seq_len), F32)
    for block in range(blocks):
        for slot in range(slots):
            hit = (row_block == block) & (column_block == pattern[block, slot])
            seen = jnp.where(hit, 1.0, seen)
    return jnp.where((row_block == column_block) & (columns > rows), 0.0, seen)


def scale_of(x):
    return lax.rsqrt(jnp.mean(x * x, axis=-1, keepdims=True) + NORM_EPS)


def attention_body(
    chunks,
    bits,
    pattern,
    x_own,
    x_mirror,
    g_own,
    g_mirror,
    w_query,
    w_key,
    w_value,
    w_out,
    attended,
    att_keep,
    att_send,
    value_keep,
    value_send,
    key_keep,
    key_send,
    query_keep,
    query_send,
    query,
    key,
    values,
    grad_att,
    turned,
):
    row_bit, col_bit = bits[0], bits[1]
    seq_len = x_own.shape[0]
    half = w_query.shape[1]
    x = jnp.concatenate([x_own[...], x_mirror[...]], axis=0)
    factor = scale_of(x.astype(F32))
    query[...] = (dot(x, w_query[...]) * factor).astype(BF16)
    key[...] = (dot(x, w_key[...]) * factor).astype(BF16)
    values[...] = (dot(x, w_value[...]) * factor).astype(BF16)
    grad = jnp.concatenate([g_own[...], g_mirror[...]], axis=0)
    grad_att[...] = dot_nt(grad, w_out[...]).astype(BF16)

    seen = seen_mask(pattern, seq_len, pattern.shape[0], pattern.shape[1])
    seen = jnp.concatenate([seen, seen], axis=0) > 0.0
    low = lax.broadcasted_iota(jnp.int32, (seq_len, PAIR), 1) < HDIM
    inv_sqrt = 1.0 / math.sqrt(HDIM)
    zero = jnp.zeros((), BF16)

    def stacked(block):
        return jnp.concatenate([jnp.where(low, block, zero), jnp.where(low, zero, block)], axis=0)

    def merged(both):
        return jnp.where(low, both[:seq_len], both[seq_len:])

    width = half // 2
    for side, outs in (
        (col_bit, (value_keep, key_keep, query_keep)),
        (1 - col_bit, (value_send, key_send, query_send)),
    ):
        for pair in range(width // PAIR):
            columns = pl.ds(pl.multiple_of(side * width + pair * PAIR, PAIR), PAIR)
            here = slice(pair * PAIR, (pair + 1) * PAIR)
            for seq in range(2):
                rows = slice(seq * seq_len, (seq + 1) * seq_len)
                q2 = stacked(query[rows, columns])
                k = key[rows, columns]
                v = values[rows, columns]
                ga2 = stacked(grad_att[rows, columns])
                r = factor[rows]
                expo = jnp.where(seen, jnp.exp(dot_nt(q2, k) * inv_sqrt), 0.0)
                prob = expo / jnp.sum(expo, axis=-1, keepdims=True)
                prob_bf = prob.astype(BF16)
                attended[rows, columns] = merged(dot(prob_bf, v)).astype(BF16)
                grad_prob = dot_nt(ga2, v)
                inner = jnp.sum(prob * grad_prob, axis=-1, keepdims=True)
                score = (prob * (grad_prob - inner) * inv_sqrt).astype(BF16)
                outs[0][rows, here] = (dot_tn(prob_bf, ga2) * r).astype(BF16)
                outs[1][rows, here] = (dot_tn(score, q2) * r).astype(BF16)
                outs[2][rows, here] = (merged(dot(score, k)) * r).astype(BF16)

    turned[...] = attended[...].astype(F32).T.astype(BF16)
    size = half // (2 * len(chunks))
    copy_chunks(turned, att_keep, chunks, size, row_bit)
    copy_chunks(turned, att_send, chunks, size, 1 - row_bit)


def returned_body(
    bits,
    x_own,
    x_mirror,
    attended,
    value_keep,
    value_send,
    key_keep,
    key_send,
    query_keep,
    query_send,
    w_query,
    w_key,
    w_value,
    w_out,
    contrib_own,
    contrib_mirror,
    returned_own,
    returned_mirror,
):
    col_bit = bits[1]
    seq_len = x_own.shape[0]
    width = value_keep.shape[1]
    contrib = dot(attended[...], w_out[...]).astype(BF16)
    contrib_own[...] = contrib[:seq_len]
    contrib_mirror[...] = contrib[seq_len:]
    keep = pl.ds(pl.multiple_of(col_bit * width, width), width)
    send = pl.ds(pl.multiple_of((1 - col_bit) * width, width), width)
    grad = dot_nt(query_keep[...], w_query[:, keep])
    grad += dot_nt(query_send[...], w_query[:, send])
    grad += dot_nt(key_keep[...], w_key[:, keep])
    grad += dot_nt(key_send[...], w_key[:, send])
    grad += dot_nt(value_keep[...], w_value[:, keep])
    grad += dot_nt(value_send[...], w_value[:, send])
    x = jnp.concatenate([x_own[...], x_mirror[...]], axis=0).astype(F32)
    factor = scale_of(x)
    mean_term = jnp.mean(x * grad, axis=-1, keepdims=True)
    returned = (grad - x * (factor * factor * mean_term)).astype(BF16)
    returned_own[...] = returned[:seq_len]
    returned_mirror[...] = returned[seq_len:]


def weight_grad_body(left_count, bits, *refs):
    first_bit = bits[2]
    lefts = refs[:left_count]
    rights = refs[left_count:-2]
    keep, send = refs[-2:]
    rows = keep.shape[0]
    right = jnp.concatenate([ref[...] for ref in rights], axis=0)
    for target, side in ((send, 1 - first_bit), (keep, first_bit)):
        part = pl.ds(pl.multiple_of(side * rows, rows), rows)
        left = jnp.concatenate([ref[part, :] for ref in lefts], axis=1)
        target[...] = dot(left, right).astype(BF16)


def on_device(hidden_in, grad_out, w_query, w_key, w_value, w_out, pattern):
    replicas = lax.axis_size("dp")
    pipe = lax.axis_size("pipe")
    bit_count = replicas.bit_length() - 1
    halved_bits = [bit for bit in range(bit_count) if bit not in (ROW_BIT, COL_BIT)]
    index = lax.axis_index("dp")
    seq_len, features = hidden_in.shape
    half = w_query.shape[2]
    w_query, w_key, w_value, w_out = w_query[0], w_key[0], w_value[0], w_out[0]

    def bit_of(bit):
        return (index >> bit) & 1

    def swap(x, bit):
        return lax.ppermute(x, "dp", [(i, i ^ (1 << bit)) for i in range(replicas)])

    def mirror(x):
        return lax.ppermute(x, "pipe", [(i, pipe - 1 - i) for i in range(pipe)])

    bits = jnp.stack([bit_of(ROW_BIT), bit_of(COL_BIT), bit_of(halved_bits[0])]).astype(jnp.int32)
    chunks = row_chunks(bit_count, halved_bits)

    def bf16(*shape):
        return jax.ShapeDtypeStruct(shape, BF16)

    x_mirror = mirror(hidden_in)
    g_mirror = mirror(grad_out)
    x_keep, x_send, g_keep, g_send = call(
        functools.partial(prep_body, chunks),
        "prep",
        (bits, hidden_in, grad_out),
        [bf16(features // 2, seq_len)] * 2 + [bf16(seq_len, features // 2)] * 2,
        [pltpu.VMEM((features, seq_len), BF16)],
    )

    def gather(keep, send, send_bit, keep_bit):
        near = swap(send, send_bit)
        far = swap(keep, keep_bit)
        last = swap(near, keep_bit)
        if send_bit == ROW_BIT:
            return [keep, near, far, last]
        return [keep, far, near, last]

    g_pieces = gather(g_keep, g_send, COL_BIT, ROW_BIT)
    x_pieces = gather(x_keep, x_send, ROW_BIT, COL_BIT)
    g_all = [piece for own in g_pieces for piece in (own, mirror(own))]
    x_all = [piece for own in x_pieces for piece in (own, mirror(own))]

    tokens = 2 * seq_len
    outs = call(
        functools.partial(attention_body, chunks),
        "attention",
        (bits, pattern, hidden_in, x_mirror, grad_out, g_mirror, w_query, w_key, w_value, w_out),
        [bf16(tokens, half)] + [bf16(half // 2, tokens)] * 2 + [bf16(tokens, half // 2)] * 6,
        [pltpu.VMEM((tokens, half), BF16)] * 4 + [pltpu.VMEM((half, tokens), BF16)],
        flops=8 * tokens * features * half,
        scalars=2,
    )
    attended, att_keep, att_send = outs[:3]
    grads = outs[3:]

    def reduced(lefts, rights, name):
        rows = lefts[0].shape[0] // 2
        columns = rights[0].shape[1]
        keep, send = call(
            functools.partial(weight_grad_body, len(lefts)),
            name,
            (bits, *lefts, *rights),
            [bf16(rows, columns)] * 2,
            flops=4 * rows * columns * tokens * 4,
        )
        for place, bit in enumerate(halved_bits):
            arrived = swap(send, bit)
            total = (keep.astype(F32) + arrived.astype(F32)).astype(BF16)
            after = halved_bits[place + 1] if place + 1 < len(halved_bits) else COL_BIT
            parts = total.reshape(2, total.shape[0] // 2, columns)
            keep = lax.dynamic_index_in_dim(parts, bit_of(after), 0, keepdims=False)
            send = lax.dynamic_index_in_dim(parts, 1 - bit_of(after), 0, keepdims=False)
        other = swap(send, COL_BIT)
        own_low = bit_of(COL_BIT) == 0
        low = jnp.where(own_low, keep, other)
        high = jnp.where(own_low, other, keep)
        return jnp.concatenate([low, high], axis=1).astype(F32)[None]

    att_pieces = gather(att_keep, att_send, ROW_BIT, COL_BIT)
    grad_wout = reduced(att_pieces, g_all, "grad_wout")
    grad_value = reduced(x_all, gather(grads[0], grads[1], COL_BIT, ROW_BIT), "grad_value")
    grad_key = reduced(x_all, gather(grads[2], grads[3], COL_BIT, ROW_BIT), "grad_key")
    grad_query = reduced(x_all, gather(grads[4], grads[5], COL_BIT, ROW_BIT), "grad_query")

    contrib, contrib_mirror, returned, returned_mirror = call(
        returned_body,
        "returned",
        (bits, hidden_in, x_mirror, attended, *grads, w_query, w_key, w_value, w_out),
        [bf16(seq_len, features)] * 4,
        flops=8 * tokens * features * half,
    )
    contrib_other = mirror(contrib_mirror)
    returned_other = mirror(returned_mirror)
    hidden_out = (
        hidden_in.astype(F32) + contrib.astype(F32) + contrib_other.astype(F32)
    ).astype(BF16)
    grad_in = (
        grad_out.astype(F32) + returned.astype(F32) + returned_other.astype(F32)
    ).astype(BF16)
    return (hidden_out, grad_in, grad_query, grad_key, grad_value, grad_wout)


def solution(mesh):
    in_specs = (
        P(("dp", "pipe"), None),
        P(("dp", "pipe"), None),
        P("pipe", None, None),
        P("pipe", None, None),
        P("pipe", None, None),
        P("pipe", None, None),
        P(),
    )
    out_specs = (
        P(("dp", "pipe"), None),
        P(("dp", "pipe"), None),
        P("pipe", "dp", None),
        P("pipe", "dp", None),
        P("pipe", "dp", None),
        P("pipe", "dp", None),
    )
    return jax.shard_map(
        on_device, mesh=mesh, in_specs=in_specs, out_specs=out_specs, check_vma=False
    )
```

```python
import functools
import math

import jax
import jax.numpy as jnp
from jax import lax
from jax.experimental import pallas as pl
from jax.experimental.pallas import tpu as pltpu
from jax.sharding import PartitionSpec as P

HDIM = 64
NORM_EPS = 1e-05
PAIR = 2 * HDIM
VMEM_BYTES = 62 * 1024 * 1024

F32 = jnp.float32
BF16 = jnp.bfloat16
NT = (((1,), (1,)), ((), ()))
TN = (((0,), (0,)), ((), ()))

ROW_BIT = 0
COL_BIT = 2

CHUNKS = ((True, (0,)), (False, (1,)), (False, (2,)))


def dot(left, right):
    return jnp.dot(left, right, preferred_element_type=F32)


def dot_nt(left, right):
    return lax.dot_general(left, right, NT, preferred_element_type=F32)


def dot_tn(left, right):
    return lax.dot_general(left, right, TN, preferred_element_type=F32)


def call(body, name, inputs, outs, scratch=(), flops=0, scalars=1, far=0):
    near = len(inputs) - scalars - far
    specs = [pl.BlockSpec(memory_space=pltpu.SMEM)] * scalars
    specs += [pl.BlockSpec(memory_space=pltpu.VMEM)] * near
    specs += [pl.BlockSpec(memory_space=pltpu.HBM)] * far
    moved = sum(x.size * x.dtype.itemsize for x in inputs)
    moved += sum(x.size * x.dtype.itemsize for x in outs)
    return pl.pallas_call(
        body,
        name=name,
        out_shape=outs,
        in_specs=specs,
        out_specs=[pl.BlockSpec(memory_space=pltpu.VMEM)] * len(outs),
        scratch_shapes=list(scratch),
        compiler_params=pltpu.CompilerParams(vmem_limit_bytes=VMEM_BYTES),
        cost_estimate=pl.CostEstimate(flops=flops, bytes_accessed=moved, transcendentals=0),
    )(*inputs)


def fetch(pairs, sems):
    copies = [
        pltpu.make_async_copy(source, target, sems.at[place])
        for place, (source, target) in enumerate(pairs)
    ]
    for copy in copies:
        copy.start()
    return copies


def finish(copies):
    for copy in copies:
        copy.wait()


def row_chunks(bit_count, halved_bits):
    order = list(halved_bits) + [COL_BIT]
    chunks = []
    for index in range(1 << len(order)):
        chunk = 0
        for place, bit in enumerate(reversed(order)):
            chunk |= ((index >> place) & 1) << bit
        chunks.append(chunk)
    return chunks


def copy_chunks(source, target, first, chunks, size, row_bit):
    for place, chunk in enumerate(chunks):
        start = pl.multiple_of((chunk + (row_bit << ROW_BIT)) * size, size)
        here = first + place * size
        target[here : here + size, :] = source[pl.ds(start, size), :]


def prep_body(
    chunks, bits, hidden, grad, keep, by_row, by_col, x, g, turned_x, turned_g, sems
):
    row_bit, col_bit = bits[0], bits[1]
    features, seq_len = turned_x.shape
    size = features // (2 * len(chunks))
    part = features // 2
    x_copy, g_copy = fetch([(hidden, x), (grad, g)], sems)
    x_copy.wait()
    turned_x[...] = x[...].astype(F32).T.astype(BF16)
    copy_chunks(turned_x, by_row, 0, chunks, size, 1 - row_bit)
    copy_chunks(turned_x, by_col, part, chunks, size, row_bit)
    g_copy.wait()
    turned_g[...] = g[...].astype(F32).T.astype(BF16)
    by_row[part:, :] = turned_g[pl.ds(pl.multiple_of(col_bit * part, part), part), :]
    by_col[:part, :] = turned_g[pl.ds(pl.multiple_of((1 - col_bit) * part, part), part), :]
    keep[:part, :] = by_col[part:, :]
    keep[part:, :] = by_row[part:, :]


def seen_mask(pattern, seq_len, blocks, slots):
    block_len = seq_len // blocks
    rows = lax.broadcasted_iota(jnp.int32, (seq_len, seq_len), 0)
    columns = lax.broadcasted_iota(jnp.int32, (seq_len, seq_len), 1)
    row_block, column_block = rows // block_len, columns // block_len
    seen = jnp.zeros((seq_len, seq_len), F32)
    for block in range(blocks):
        for slot in range(slots):
            hit = (row_block == block) & (column_block == pattern[block, slot])
            seen = jnp.where(hit, 1.0, seen)
    return jnp.where((row_block == column_block) & (columns > rows), 0.0, seen)


def scale_of(x):
    return lax.rsqrt(jnp.mean(x * x, axis=-1, keepdims=True) + NORM_EPS)


def attention_body(
    chunks,
    bits,
    pattern,
    x_own,
    x_mirror,
    w_query,
    w_key,
    w_value,
    g_own,
    g_mirror,
    w_out,
    attended,
    *rest,
):
    sends = rest[: 2 * len(CHUNKS)]
    x_all, weights, weight_out, g_all, query, key, values, grad_att, turned, sems = rest[
        2 * len(CHUNKS) :
    ]
    row_bit, col_bit = bits[0], bits[1]
    seq_len = x_own.shape[0]
    tokens = 2 * seq_len
    half = w_query.shape[1]
    own, other = pl.ds(0, seq_len), pl.ds(seq_len, seq_len)
    copies = fetch(
        [
            (x_own, x_all.at[own]),
            (x_mirror, x_all.at[other]),
            (w_query, weights.at[0]),
            (w_key, weights.at[1]),
            (w_value, weights.at[2]),
            (g_own, g_all.at[own]),
            (g_mirror, g_all.at[other]),
            (w_out, weight_out),
        ],
        sems,
    )
    finish(copies[:2])
    x = x_all[...]
    factor = scale_of(x.astype(F32))
    for place, target in enumerate((query, key, values)):
        copies[2 + place].wait()
        target[...] = (dot(x, weights[place]) * factor).astype(BF16)
    finish(copies[5:])
    grad_att[...] = dot_nt(g_all[...], weight_out[...]).astype(BF16)

    seen = seen_mask(pattern, seq_len, pattern.shape[0], pattern.shape[1])
    seen = jnp.concatenate([seen, seen], axis=0) > 0.0
    low = lax.broadcasted_iota(jnp.int32, (seq_len, PAIR), 1) < HDIM
    inv_sqrt = 1.0 / math.sqrt(HDIM)
    zero = jnp.zeros((), BF16)

    def stacked(block):
        return jnp.concatenate([jnp.where(low, block, zero), jnp.where(low, zero, block)], axis=0)

    def merged(both):
        return jnp.where(low, both[:seq_len], both[seq_len:])

    width = half // 2
    places = {}
    att_place = None
    for (has_out, members), by_row, by_col in zip(CHUNKS, sends[::2], sends[1::2]):
        for place, member in enumerate(members):
            places[member] = (by_row, by_col, place * tokens)
        if has_out:
            att_place = (by_row, by_col, len(members) * tokens)

    for outs_at, side in ((0, col_bit), (1, 1 - col_bit)):
        for pair in range(width // PAIR):
            columns = pl.ds(pl.multiple_of(side * width + pair * PAIR, PAIR), PAIR)
            here = slice(pair * PAIR, (pair + 1) * PAIR)
            for seq in range(2):
                rows = slice(seq * seq_len, (seq + 1) * seq_len)
                q2 = stacked(query[rows, columns])
                k = key[rows, columns]
                v = values[rows, columns]
                ga2 = stacked(grad_att[rows, columns])
                r = factor[rows]

                def put(member, value):
                    target, first = places[member][outs_at], places[member][2] + seq * seq_len
                    target[first : first + seq_len, here] = (value * r).astype(BF16)

                expo = jnp.where(seen, jnp.exp(dot_nt(q2, k) * inv_sqrt), 0.0)
                prob = expo / jnp.sum(expo, axis=-1, keepdims=True)
                prob_bf = prob.astype(BF16)
                attended[rows, columns] = merged(dot(prob_bf, v)).astype(BF16)
                grad_prob = dot_nt(ga2, v)
                inner = jnp.sum(prob * grad_prob, axis=-1, keepdims=True)
                score = (prob * (grad_prob - inner) * inv_sqrt).astype(BF16)
                put(0, dot_tn(prob_bf, ga2))
                put(1, dot_tn(score, q2))
                put(2, merged(dot(score, k)))

    turned[...] = attended[...].astype(F32).T.astype(BF16)
    size = half // (2 * len(chunks))
    copy_chunks(turned, att_place[0], att_place[2], chunks, size, 1 - row_bit)
    copy_chunks(turned, att_place[1], att_place[2], chunks, size, row_bit)


def returned_body(bits, x_own, x_mirror, attended, w_out, w_query, w_key, w_value, *rest):
    sends = rest[: 2 * len(CHUNKS)]
    contrib_own, contrib_mirror, returned_own, returned_mirror = rest[
        2 * len(CHUNKS) : 2 * len(CHUNKS) + 4
    ]
    x_all, att, weight_out, weights, grads, sems = rest[2 * len(CHUNKS) + 4 :]
    col_bit = bits[1]
    seq_len = x_own.shape[0]
    tokens, half = att.shape
    width = half // 2
    keep = pl.ds(pl.multiple_of(col_bit * width, width), width)
    send = pl.ds(pl.multiple_of((1 - col_bit) * width, width), width)
    pairs = [
        (attended, att),
        (w_out, weight_out),
        (x_own, x_all.at[pl.ds(0, seq_len)]),
        (x_mirror, x_all.at[pl.ds(seq_len, seq_len)]),
    ]
    for (_, members), by_row, by_col in zip(CHUNKS, sends[::2], sends[1::2]):
        for place, member in enumerate(members):
            rows = pl.ds(place * tokens, tokens)
            pairs.append((by_row.at[rows], grads.at[member, :, keep]))
            pairs.append((by_col.at[rows], grads.at[member, :, send]))
    pairs += [(w_value, weights.at[0]), (w_key, weights.at[1]), (w_query, weights.at[2])]
    copies = fetch(pairs, sems)
    finish(copies[:2])
    contrib = dot(att[...], weight_out[...]).astype(BF16)
    contrib_own[...] = contrib[:seq_len]
    contrib_mirror[...] = contrib[seq_len:]
    finish(copies[2:-3])
    grad = None
    for member in range(3):
        copies[member - 3].wait()
        term = dot_nt(grads[member], weights[member])
        grad = term if grad is None else grad + term
    x = x_all[...].astype(F32)
    factor = scale_of(x)
    mean_term = jnp.mean(x * grad, axis=-1, keepdims=True)
    returned = (grad - x * (factor * factor * mean_term)).astype(BF16)
    returned_own[...] = returned[:seq_len]
    returned_mirror[...] = returned[seq_len:]


def weight_grad_body(chunk, size, out_size, bits, *refs):
    has_out, members = chunk
    x_pieces, refs = refs[:8], refs[8:]
    g_pieces, refs = refs[:4], refs[4:]
    if has_out:
        out_pieces, att_pieces, refs = refs[:8], refs[8:12], refs[12:]
        send, keep, x_all, right, att, out_right, sems = refs
    else:
        send, keep, x_all, right, sems = refs
    width = send.shape[1]
    count = len(members)
    seq_len = x_all.shape[1] // 8
    tokens = 2 * seq_len
    rows = x_all.shape[0] // 2
    first_bit = bits[2]
    pairs = []

    def add(ref, first, extent, target):
        pairs.append((ref.at[pl.ds(first, extent)], target))

    for place, (ref, first) in enumerate(x_pieces):
        add(ref, first, 2 * rows, x_all.at[:, pl.ds(place * seq_len, seq_len)])
    for place, (ref, first) in enumerate(g_pieces):
        for at in range(count):
            target = right.at[pl.ds(place * tokens, tokens), pl.ds(at * width, width)]
            add(ref, first + at * tokens, tokens, target)
    if has_out:
        for place, (ref, first) in enumerate(out_pieces):
            add(ref, first, out_right.shape[0], out_right.at[:, pl.ds(place * seq_len, seq_len)])
        for place, (ref, first) in enumerate(att_pieces):
            add(ref, first, att.shape[0], att.at[:, pl.ds(place * tokens, tokens)])
    finish(fetch(pairs, sems))

    finals = rows // size
    blocks = out_right.shape[0] // width if has_out else 0
    total = count * size + blocks * out_size
    for target, side in ((send, 1 - first_bit), (keep, first_bit)):
        if count:
            part = pl.ds(pl.multiple_of(side * rows, rows), rows)
            grad = dot(x_all[part, :], right[...]).astype(BF16)
            for final in range(finals):
                for at in range(count):
                    first = final * total + at * size
                    target[first : first + size, :] = grad[
                        final * size : (final + 1) * size, at * width : (at + 1) * width
                    ]
        if has_out:
            out_rows = att.shape[0] // 2
            part = pl.ds(pl.multiple_of(side * out_rows, out_rows), out_rows)
            grad = dot_nt(att[part, :], out_right[...]).astype(BF16)
            for final in range(finals):
                for block in range(blocks):
                    first = final * total + count * size + block * out_size
                    target[first : first + out_size, :] = grad[
                        final * out_size : (final + 1) * out_size,
                        block * width : (block + 1) * width,
                    ]


def on_device(hidden_in, grad_out, w_query, w_key, w_value, w_out, pattern):
    replicas = lax.axis_size("dp")
    pipe = lax.axis_size("pipe")
    bit_count = replicas.bit_length() - 1
    halved_bits = [bit for bit in range(bit_count) if bit not in (ROW_BIT, COL_BIT)]
    index = lax.axis_index("dp")
    seq_len, features = hidden_in.shape
    half = w_query.shape[2]
    w_query, w_key, w_value, w_out = w_query[0], w_key[0], w_value[0], w_out[0]

    def bit_of(bit):
        return (index >> bit) & 1

    def swap(x, bit):
        return lax.ppermute(x, "dp", [(i, i ^ (1 << bit)) for i in range(replicas)])

    def mirror(x):
        return lax.ppermute(x, "pipe", [(i, pipe - 1 - i) for i in range(pipe)])

    bits = jnp.stack([bit_of(ROW_BIT), bit_of(COL_BIT), bit_of(halved_bits[0])]).astype(jnp.int32)
    chunks = row_chunks(bit_count, halved_bits)

    def bf16(*shape):
        return jax.ShapeDtypeStruct(shape, BF16)

    width = half // 2
    part = features // 2
    tokens = 2 * seq_len
    size = features // replicas
    out_size = half // replicas

    x_mirror = mirror(hidden_in)
    g_mirror = mirror(grad_out)
    own, by_row, by_col = call(
        functools.partial(prep_body, chunks),
        "prep",
        (bits, hidden_in, grad_out),
        [bf16(features, seq_len)] * 3,
        [pltpu.VMEM((seq_len, features), BF16)] * 2
        + [pltpu.VMEM((features, seq_len), BF16)] * 2
        + [pltpu.SemaphoreType.DMA((2,))],
        far=2,
    )
    from_row = swap(by_row, ROW_BIT)
    from_col = swap(by_col, COL_BIT)
    own_mirror = mirror(own)
    x_last = swap(from_row[:part], COL_BIT)
    g_last = swap(from_col[:part], ROW_BIT)
    row_mirror, col_mirror = mirror(from_row), mirror(from_col)
    x_last_mirror, g_last_mirror = mirror(x_last), mirror(g_last)
    x_pieces = [(own, 0), (own_mirror, 0), (from_row, 0), (row_mirror, 0)]
    x_pieces += [(from_col, part), (col_mirror, part), (x_last, 0), (x_last_mirror, 0)]
    out_pieces = [(own, part), (own_mirror, part), (from_row, part), (row_mirror, part)]
    out_pieces += [(from_col, 0), (col_mirror, 0), (g_last, 0), (g_last_mirror, 0)]

    heights = [(len(members) + has_out) * tokens for has_out, members in CHUNKS]
    attended, *sends = call(
        functools.partial(attention_body, chunks),
        "attention",
        (bits, pattern, hidden_in, x_mirror, w_query, w_key, w_value, grad_out, g_mirror, w_out),
        [bf16(tokens, half)] + [bf16(height, width) for height in heights for _ in range(2)],
        [
            pltpu.VMEM((tokens, features), BF16),
            pltpu.VMEM((3, features, half), BF16),
            pltpu.VMEM((half, features), BF16),
            pltpu.VMEM((tokens, features), BF16),
        ]
        + [pltpu.VMEM((tokens, half), BF16)] * 4
        + [pltpu.VMEM((half, tokens), BF16), pltpu.SemaphoreType.DMA((8,))],
        flops=8 * tokens * features * half,
        scalars=2,
        far=8,
    )

    def exchanged(chunk, by_row, by_col):
        has_out, members = chunk
        height = len(members) * tokens
        from_row = swap(by_row, ROW_BIT)
        from_col = swap(by_col, COL_BIT)
        g_pieces, att_pieces = [], []
        if members:
            last = swap(from_col[:height], ROW_BIT)
            g_pieces = [(by_row, 0), (from_row, 0), (from_col, 0), (last, 0)]
        if has_out:
            last = swap(from_row[height:], COL_BIT)
            att_pieces = [(by_col, height), (from_row, height), (from_col, height), (last, 0)]
        return g_pieces, att_pieces

    def product(chunk, g_pieces, att_pieces):
        has_out, members = chunk
        pieces = list(x_pieces) + g_pieces
        if has_out:
            pieces += out_pieces + att_pieces
        arrays = []
        for array, _ in pieces:
            if not any(array is known for known in arrays):
                arrays.append(array)
        places = [
            ([array is known for known in arrays].index(True), first) for array, first in pieces
        ]
        blocks = part // width if has_out else 0
        height = (part // 2 // size) * (len(members) * size + blocks * out_size)
        scratch = [
            pltpu.VMEM((part, 8 * seq_len), BF16),
            pltpu.VMEM((8 * seq_len, len(members) * width), BF16),
        ]
        if has_out:
            scratch += [pltpu.VMEM((width, 8 * seq_len), BF16)]
            scratch += [pltpu.VMEM((part, 8 * seq_len), BF16)]
        scratch += [pltpu.SemaphoreType.DMA((8 + 4 * len(members) + 12 * has_out,))]

        def body(bits, *refs):
            inputs = [(refs[place], first) for place, first in places]
            weight_grad_body(chunk, size, out_size, bits, *inputs, *refs[len(arrays) :])

        return call(
            body,
            "weight_grad",
            (bits, *arrays),
            [bf16(height, width)] * 2,
            scratch,
            flops=16 * seq_len * part * width * (len(members) + has_out),
            far=len(arrays),
        )

    def halved(send, keep):
        for place, bit in enumerate(halved_bits):
            arrived = swap(send, bit)
            total = (keep.astype(F32) + arrived.astype(F32)).astype(BF16)
            after = halved_bits[place + 1] if place + 1 < len(halved_bits) else COL_BIT
            parts = total.reshape(2, total.shape[0] // 2, width)
            keep = lax.dynamic_index_in_dim(parts, bit_of(after), 0, keepdims=False)
            send = lax.dynamic_index_in_dim(parts, 1 - bit_of(after), 0, keepdims=False)
        return send, keep

    def placed(chunk, send, keep):
        has_out, members = chunk
        other = swap(send, COL_BIT)
        own_low = bit_of(COL_BIT) == 0
        low = jnp.where(own_low, keep, other)
        high = jnp.where(own_low, other, keep)
        found = {}
        for at, member in enumerate(members):
            rows = slice(at * size, (at + 1) * size)
            found[member] = jnp.concatenate([low[rows], high[rows]], axis=1).astype(F32)[None]
        if has_out:
            first = len(members) * size
            blocks = [
                side[first + at * out_size : first + (at + 1) * out_size]
                for side in (low, high)
                for at in range(part // width)
            ]
            found["out"] = jnp.concatenate(blocks, axis=1).astype(F32)[None]
        return found

    pieces = [exchanged(chunk, *sends[2 * at : 2 * at + 2]) for at, chunk in enumerate(CHUNKS)]
    products = [product(chunk, *piece) for chunk, piece in zip(CHUNKS, pieces)]

    contrib, contrib_mirror, returned, returned_mirror = call(
        returned_body,
        "returned",
        (bits, hidden_in, x_mirror, attended, w_out, w_query, w_key, w_value, *sends),
        [bf16(seq_len, features)] * 4,
        [
            pltpu.VMEM((tokens, features), BF16),
            pltpu.VMEM((tokens, half), BF16),
            pltpu.VMEM((half, features), BF16),
            pltpu.VMEM((3, features, half), BF16),
            pltpu.VMEM((3, tokens, half), BF16),
            pltpu.SemaphoreType.DMA((13,)),
        ],
        flops=8 * tokens * features * half,
        far=7 + len(sends),
    )
    found = {}
    for chunk, (send, keep) in zip(CHUNKS, products):
        found |= placed(chunk, *halved(send, keep))
    contrib_other = mirror(contrib_mirror)
    returned_other = mirror(returned_mirror)
    hidden_out = (
        hidden_in.astype(F32) + contrib.astype(F32) + contrib_other.astype(F32)
    ).astype(BF16)
    grad_in = (
        grad_out.astype(F32) + returned.astype(F32) + returned_other.astype(F32)
    ).astype(BF16)
    return (hidden_out, grad_in, found[2], found[1], found[0], found["out"])


def solution(mesh):
    in_specs = (
        P(("dp", "pipe"), None),
        P(("dp", "pipe"), None),
        P("pipe", None, None),
        P("pipe", None, None),
        P("pipe", None, None),
        P("pipe", None, None),
        P(),
    )
    out_specs = (
        P(("dp", "pipe"), None),
        P(("dp", "pipe"), None),
        P("pipe", "dp", None),
        P("pipe", "dp", None),
        P("pipe", "dp", None),
        P("pipe", "dp", None),
    )
    return jax.shard_map(
        on_device, mesh=mesh, in_specs=in_specs, out_specs=out_specs, check_vma=False
    )
```

```python
import functools
import math

import jax
import jax.numpy as jnp
from jax import lax
from jax.experimental import pallas as pl
from jax.experimental.pallas import tpu as pltpu
from jax.sharding import PartitionSpec as P

HDIM = 64
NORM_EPS = 1e-05
PAIR = 2 * HDIM
VMEM_BYTES = 62 * 1024 * 1024

ATTENTION_WORK = 11 * 10**9

F32 = jnp.float32
BF16 = jnp.bfloat16
NT = (((1,), (1,)), ((), ()))
TN = (((0,), (0,)), ((), ()))

PROJECTION_BITS = (0, 1)
OUT_BIT = 2

UNITS = ((0, 1), (2,))


def dot(left, right):
    return jnp.dot(left, right, preferred_element_type=F32)


def dot_nt(left, right):
    return lax.dot_general(left, right, NT, preferred_element_type=F32)


def dot_tn(left, right):
    return lax.dot_general(left, right, TN, preferred_element_type=F32)


def call(body, name, inputs, outs, scratch=(), work=0, scalars=0, far=0, after=()):
    near = len(inputs) - scalars - far
    count = len(inputs)
    specs = [pl.BlockSpec(memory_space=pltpu.SMEM)] * scalars
    specs += [pl.BlockSpec(memory_space=pltpu.VMEM)] * near
    specs += [pl.BlockSpec(memory_space=pltpu.HBM)] * (far + len(after))

    def run(*refs):
        body(*refs[:count], *refs[count + len(after) :])

    return pl.pallas_call(
        run,
        name=name,
        out_shape=outs,
        in_specs=specs,
        out_specs=[pl.BlockSpec(memory_space=pltpu.VMEM)] * len(outs),
        scratch_shapes=list(scratch),
        compiler_params=pltpu.CompilerParams(vmem_limit_bytes=VMEM_BYTES),
        cost_estimate=pl.CostEstimate(flops=work, bytes_accessed=0, transcendentals=0),
    )(*inputs, *after)


def fetch(pairs, sems):
    copies = [
        pltpu.make_async_copy(source, target, sems.at[place])
        for place, (source, target) in enumerate(pairs)
    ]
    for copy in copies:
        copy.start()
    return copies


def finish(copies):
    for copy in copies:
        copy.wait()


def spread(bits):
    found = [0]
    for bit in bits:
        found = [index | (value << bit) for index in found for value in (0, 1)]
    return found


def groups(bits, bit_count):
    others = [bit for bit in range(bit_count) if bit not in bits]
    return [[base | part for part in spread(bits)] for base in spread(others)]


def copy_chunks(source, target, chunks, size):
    for place, chunk in enumerate(chunks):
        target[place * size : (place + 1) * size, :] = source[chunk * size : (chunk + 1) * size, :]


def bit_here(bit):
    return (lax.axis_index("dp") >> bit) & 1


def prep_body(chunks, hidden, grad, x_blocks, g_send, x, turned, sems):
    columns = g_send.shape[1]
    away = pl.ds(pl.multiple_of((1 - bit_here(OUT_BIT)) * columns, columns), columns)
    x_copy, g_copy = fetch([(hidden, x), (grad.at[:, away], g_send)], sems)
    x_copy.wait()
    turned[...] = x[...].astype(F32).T.astype(BF16)
    for member in range(4):
        own = [chunk | (member % 2) << PROJECTION_BITS[0] for chunk in chunks]
        copy_chunks(turned, x_blocks.at[member], own, turned.shape[0] // (2 * len(own)))
    g_copy.wait()


def seen_mask(pattern, seq_len, blocks, slots):
    block_len = seq_len // blocks
    rows = lax.broadcasted_iota(jnp.int32, (seq_len, seq_len), 0)
    columns = lax.broadcasted_iota(jnp.int32, (seq_len, seq_len), 1)
    row_block, column_block = rows // block_len, columns // block_len
    seen = jnp.zeros((seq_len, seq_len), F32)
    for block in range(blocks):
        for slot in range(slots):
            hit = (row_block == block) & (column_block == pattern[block, slot])
            seen = jnp.where(hit, 1.0, seen)
    return jnp.where((row_block == column_block) & (columns > rows), 0.0, seen)


def scale_of(x):
    return lax.rsqrt(jnp.mean(x * x, axis=-1, keepdims=True) + NORM_EPS)


def attention_body(
    out_chunks,
    pattern,
    x_own,
    x_mirror,
    w_query,
    w_key,
    w_value,
    g_own,
    g_mirror,
    w_out,
    attended,
    att_turned,
    blocks,
    x_all,
    weights,
    weight_out,
    g_all,
    query,
    key,
    values,
    grad_att,
    turned,
    sems,
):
    seq_len = x_own.shape[0]
    tokens = 2 * seq_len
    half = w_query.shape[1]
    own, other = pl.ds(0, seq_len), pl.ds(seq_len, seq_len)
    copies = fetch(
        [
            (x_own, x_all.at[own]),
            (x_mirror, x_all.at[other]),
            (w_query, weights.at[0]),
            (w_key, weights.at[1]),
            (w_value, weights.at[2]),
            (g_own, g_all.at[own]),
            (g_mirror, g_all.at[other]),
            (w_out, weight_out),
        ],
        sems,
    )
    finish(copies[:2])
    x = x_all[...]
    factor = scale_of(x.astype(F32))
    for place, target in enumerate((query, key, values)):
        copies[2 + place].wait()
        target[...] = (dot(x, weights[place]) * factor).astype(BF16)
    finish(copies[5:])
    grad_att[...] = dot_nt(g_all[...], weight_out[...]).astype(BF16)

    seen = seen_mask(pattern, seq_len, pattern.shape[0], pattern.shape[1])
    seen = jnp.concatenate([seen, seen], axis=0) > 0.0
    low = lax.broadcasted_iota(jnp.int32, (seq_len, PAIR), 1) < HDIM
    inv_sqrt = 1.0 / math.sqrt(HDIM)
    zero = jnp.zeros((), BF16)

    def stacked(block):
        return jnp.concatenate([jnp.where(low, block, zero), jnp.where(low, zero, block)], axis=0)

    def merged(both):
        return jnp.where(low, both[:seq_len], both[seq_len:])

    width = half // 2
    def put(member, col, first, here, value):
        rounded = value.astype(BF16)
        first += member * tokens
        for row in range(2):
            blocks[2 * col + row, first : first + seq_len, here] = rounded

    for pair in range(half // PAIR):
        columns = slice(pair * PAIR, (pair + 1) * PAIR)
        col, start = pair * PAIR // width, pair * PAIR % width
        here = slice(start, start + PAIR)
        for seq in range(2):
            rows = slice(seq * seq_len, (seq + 1) * seq_len)
            q2 = stacked(query[rows, columns])
            k = key[rows, columns]
            v = values[rows, columns]
            ga2 = stacked(grad_att[rows, columns])
            r = factor[rows]

            expo = jnp.where(seen, jnp.exp(dot_nt(q2, k) * inv_sqrt), 0.0)
            prob = expo / jnp.sum(expo, axis=-1, keepdims=True)
            prob_bf = prob.astype(BF16)
            attended[rows, columns] = merged(dot(prob_bf, v)).astype(BF16)
            grad_prob = dot_nt(ga2, v)
            inner = jnp.sum(prob * grad_prob, axis=-1, keepdims=True)
            score = (prob * (grad_prob - inner) * inv_sqrt).astype(BF16)
            put(0, col, seq * seq_len, here, dot_tn(prob_bf, ga2) * r)
            put(1, col, seq * seq_len, here, dot_tn(score, q2) * r)
            put(2, col, seq * seq_len, here, merged(dot(score, k)) * r)

    turned[...] = attended[...].astype(F32).T.astype(BF16)
    copy_chunks(turned, att_turned, out_chunks, half // len(out_chunks))


def returned_body(
    x_own,
    x_mirror,
    attended,
    w_out,
    w_query,
    w_key,
    w_value,
    blocks,
    contrib_own,
    contrib_mirror,
    returned_own,
    returned_mirror,
    x_all,
    att,
    weight_out,
    weights,
    grads,
    sems,
):
    seq_len = x_own.shape[0]
    tokens, half = att.shape
    width = half // 2
    pairs = [
        (attended, att),
        (w_out, weight_out),
        (x_own, x_all.at[pl.ds(0, seq_len)]),
        (x_mirror, x_all.at[pl.ds(seq_len, seq_len)]),
    ]
    for member in range(3):
        for col in range(2):
            source = blocks.at[2 * col, pl.ds(member * tokens, tokens)]
            pairs.append((source, grads.at[member, :, pl.ds(col * width, width)]))
    pairs += [(w_value, weights.at[0]), (w_key, weights.at[1]), (w_query, weights.at[2])]
    copies = fetch(pairs, sems)
    finish(copies[:2])
    contrib = dot(att[...], weight_out[...]).astype(BF16)
    contrib_own[...] = contrib[:seq_len]
    contrib_mirror[...] = contrib[seq_len:]
    finish(copies[2:-3])
    grad = None
    for member in range(3):
        copies[member - 3].wait()
        term = dot_nt(grads[member], weights[member])
        grad = term if grad is None else grad + term
    x = x_all[...].astype(F32)
    factor = scale_of(x)
    mean_term = jnp.mean(x * grad, axis=-1, keepdims=True)
    returned = (grad - x * (factor * factor * mean_term)).astype(BF16)
    returned_own[...] = returned[:seq_len]
    returned_mirror[...] = returned[seq_len:]


def projection_grad_body(first_bit, x_pieces, x_mirrors, g_pieces, *rest):
    targets, (x_all, right, sems) = rest[: 2 * len(UNITS)], rest[2 * len(UNITS) :]
    seq_len = x_pieces.shape[2]
    tokens = 2 * seq_len
    width = g_pieces.shape[2]
    members = [member for unit in UNITS for member in unit]
    pairs = []
    for place in range(4):
        for at, source in enumerate((x_pieces, x_mirrors)):
            columns = pl.ds(place * tokens + at * seq_len, seq_len)
            pairs.append((source.at[place], x_all.at[:, columns]))
        for at, member in enumerate(members):
            target = right.at[pl.ds(place * tokens, tokens), pl.ds(at * width, width)]
            pairs.append((g_pieces.at[place, pl.ds(member * tokens, tokens)], target))
    finish(fetch(pairs, sems))
    bit = bit_here(first_bit)
    rows = x_all.shape[0] // 2
    for turn, side in ((0, 1 - bit), (1, bit)):
        part = pl.ds(pl.multiple_of(side * rows, rows), rows)
        column = 0
        for unit in range(len(UNITS)):
            target = targets[2 * unit + turn]
            columns = slice(column, column + target.shape[1])
            target[...] = dot(x_all[part, :], right[:, columns]).astype(BF16)
            column += target.shape[1]


def add_body(keep, arrived, total):
    total[...] = (keep[...].astype(F32) + arrived[...].astype(F32)).astype(BF16)


def out_grad_body(
    first_bit, grad, g_mirror, g_piece, g_piece_mirror, att_own, att_piece, send, keep, *scratch
):
    left, right, sems = scratch
    seq_len = grad.shape[0]
    tokens = 2 * seq_len
    columns = right.shape[1]
    here = pl.ds(pl.multiple_of(bit_here(OUT_BIT) * columns, columns), columns)
    pairs = [
        (att_own, left.at[:, pl.ds(0, tokens)]),
        (att_piece, left.at[:, pl.ds(tokens, tokens)]),
    ]
    for place, source in enumerate(
        (grad.at[:, here], g_mirror.at[:, here], g_piece, g_piece_mirror)
    ):
        pairs.append((source, right.at[pl.ds(place * seq_len, seq_len)]))
    finish(fetch(pairs, sems))
    bit = bit_here(first_bit)
    rows = left.shape[0] // 2
    for target, side in ((send, 1 - bit), (keep, bit)):
        part = pl.ds(pl.multiple_of(side * rows, rows), rows)
        target[...] = dot(left[part, :], right[...]).astype(BF16)


def final_body(count, pieces, *targets):
    width = pieces.shape[2] // count
    for at, target in enumerate(targets):
        here = slice(at * width, (at + 1) * width)
        for col in range(2):
            total = pieces[col, :, here].astype(F32)
            for place in range(1, pieces.shape[0] // 2):
                total += pieces[2 * place + col, :, here].astype(F32)
            target[:, col * width : (col + 1) * width] = total


def halve_body(bit, keep, arrived, send, next_keep):
    here = bit_here(bit)
    rows = send.shape[0]
    for target, side in ((send, 1 - here), (next_keep, here)):
        part = pl.ds(pl.multiple_of(side * rows, rows), rows)
        total = keep[part, :].astype(F32) + arrived[part, :].astype(F32)
        target[...] = total.astype(BF16)


def on_device(hidden_in, grad_out, w_query, w_key, w_value, w_out, pattern):
    replicas = lax.axis_size("dp")
    pipe = lax.axis_size("pipe")
    bit_count = replicas.bit_length() - 1
    row_bit, col_bit = PROJECTION_BITS
    halved_bits = [bit for bit in range(bit_count) if bit not in PROJECTION_BITS]
    out_bits = [col_bit, row_bit] + [bit for bit in halved_bits if bit != OUT_BIT]
    chunks = spread(halved_bits + [col_bit])
    out_chunks = spread(out_bits + [OUT_BIT])
    seq_len, features = hidden_in.shape
    half = w_query.shape[2]
    w_query, w_key, w_value, w_out = w_query[0], w_key[0], w_value[0], w_out[0]
    width, part, tokens = half // 2, features // 2, 2 * seq_len

    def swap(x, *bits):
        apart = sum(1 << bit for bit in bits)
        return lax.ppermute(x, "dp", [(i, i ^ apart) for i in range(replicas)])

    def mirror(x):
        return lax.ppermute(x, "pipe", [(i, pipe - 1 - i) for i in range(pipe)])

    def exchange(x, bits):
        members = groups(bits, bit_count)
        return lax.all_to_all(x, "dp", 0, 0, axis_index_groups=members, tiled=True)

    def follows(x, before):
        return lax.optimization_barrier((x, before))[0]

    def bf16(*shape):
        return jax.ShapeDtypeStruct(shape, BF16)

    x_mirror = mirror(hidden_in)
    g_mirror = mirror(grad_out)
    x_blocks, g_send = call(
        functools.partial(prep_body, chunks),
        "prep",
        (hidden_in, grad_out),
        [bf16(4, part, seq_len), bf16(seq_len, part)],
        [
            pltpu.VMEM((seq_len, features), BF16),
            pltpu.VMEM((features, seq_len), BF16),
            pltpu.SemaphoreType.DMA((2,)),
        ],
        far=2,
    )
    x_pieces = exchange(x_blocks, [col_bit, row_bit])
    g_piece = swap(g_send, OUT_BIT)

    attended, att_turned, g_blocks = call(
        functools.partial(attention_body, out_chunks),
        "attention",
        (pattern, hidden_in, x_mirror, w_query, w_key, w_value, grad_out, g_mirror, w_out),
        [bf16(tokens, half), bf16(half, tokens)]
        + [bf16(4, 3 * tokens, width)],
        [
            pltpu.VMEM((tokens, features), BF16),
            pltpu.VMEM((3, features, half), BF16),
            pltpu.VMEM((half, features), BF16),
            pltpu.VMEM((tokens, features), BF16),
        ]
        + [pltpu.VMEM((tokens, half), BF16)] * 4
        + [
            pltpu.VMEM((half, tokens), BF16),
            pltpu.SemaphoreType.DMA((8,)),
        ],
        work=ATTENTION_WORK,
        scalars=1,
        far=8,
        after=(x_blocks,),
    )
    g_pieces = exchange(follows(g_blocks, g_piece), [col_bit, row_bit])
    att_piece = swap(att_turned, OUT_BIT)
    x_mirrors = mirror(follows(x_pieces, attended))
    g_piece_mirror = mirror(follows(g_piece, attended))

    contrib, contrib_mirror, returned, returned_mirror = call(
        returned_body,
        "returned",
        (hidden_in, x_mirror, attended, w_out, w_query, w_key, w_value, g_blocks),
        [bf16(seq_len, features)] * 4,
        [
            pltpu.VMEM((tokens, features), BF16),
            pltpu.VMEM((tokens, half), BF16),
            pltpu.VMEM((half, features), BF16),
            pltpu.VMEM((3, features, half), BF16),
            pltpu.VMEM((3, tokens, half), BF16),
            pltpu.SemaphoreType.DMA((13,)),
        ],
        far=8,
    )

    out_send, out_keep = call(
        functools.partial(out_grad_body, out_bits[0]),
        "out_grad",
        (grad_out, g_mirror, g_piece, g_piece_mirror, att_turned, att_piece),
        [bf16(half // 2, part)] * 2,
        [
            pltpu.VMEM((half, 2 * tokens), BF16),
            pltpu.VMEM((2 * tokens, part), BF16),
            pltpu.SemaphoreType.DMA((6,)),
        ],
        far=6,
        after=(contrib,),
    )
    parts = call(
        functools.partial(projection_grad_body, halved_bits[0]),
        "projection_grad",
        (x_pieces, x_mirrors, g_pieces),
        [bf16(part // 2, len(unit) * width) for unit in UNITS for _ in range(2)],
        [
            pltpu.VMEM((part, 4 * tokens), BF16),
            pltpu.VMEM((4 * tokens, 3 * width), BF16),
            pltpu.SemaphoreType.DMA((20,)),
        ],
        far=3,
        after=(out_send,),
    )
    last_parts = parts[0]

    def halve(place, send, keep, after):
        return call(
            functools.partial(halve_body, (out_bits + [OUT_BIT])[place + 1]),
            "halve",
            (keep, swap(send, out_bits[place])),
            [bf16(keep.shape[0] // 2, part)] * 2,
            after=(after,),
        )

    def add(unit, after):
        send, keep = parts[2 * unit : 2 * unit + 2]
        return call(
            add_body,
            "add",
            (keep, swap(send, halved_bits[0])),
            [bf16(*keep.shape)],
            after=(after,),
        )[0]

    def finals(unit, total, after):
        pieces = exchange(total, halved_bits[1:] + [col_bit])
        members = UNITS[unit]
        return call(
            functools.partial(final_body, len(members)),
            "final",
            (pieces.reshape(2 << (len(halved_bits) - 1), -1, total.shape[1]),),
            [jax.ShapeDtypeStruct((features // replicas, half), F32)] * len(members),
            after=(after,),
        )

    totals = []
    last = parts[0]
    for unit in range(len(UNITS)):
        totals.append(add(unit, last))
        out_send, out_keep = halve(unit, out_send, out_keep, totals[-1])
        last = out_send
    found = {}
    for unit, members in enumerate(UNITS):
        grads = finals(unit, totals[unit], last)
        found |= {member: grad[None] for member, grad in zip(members, grads)}
        if len(UNITS) + unit < len(out_bits):
            out_send, out_keep = halve(len(UNITS) + unit, out_send, out_keep, grads[0])
            last = out_send
    for place in range(2 * len(UNITS), len(out_bits)):
        out_send, out_keep = halve(place, out_send, out_keep, last)
    out_other = swap(out_send, OUT_BIT)
    own_low = (lax.axis_index("dp") >> OUT_BIT) & 1 == 0
    low = jnp.where(own_low, out_keep, out_other)
    high = jnp.where(own_low, out_other, out_keep)
    grad_wout = jnp.concatenate([low, high], axis=1).astype(F32)[None]

    contrib_other = mirror(follows(contrib_mirror, parts[0]))
    returned_other = mirror(follows(returned_mirror, last_parts))
    hidden_out = (
        hidden_in.astype(F32) + contrib.astype(F32) + contrib_other.astype(F32)
    ).astype(BF16)
    grad_in = (
        grad_out.astype(F32) + returned.astype(F32) + returned_other.astype(F32)
    ).astype(BF16)
    return (hidden_out, grad_in, found[2], found[1], found[0], grad_wout)


def solution(mesh):
    in_specs = (
        P(("dp", "pipe"), None),
        P(("dp", "pipe"), None),
        P("pipe", None, None),
        P("pipe", None, None),
        P("pipe", None, None),
        P("pipe", None, None),
        P(),
    )
    out_specs = (
        P(("dp", "pipe"), None),
        P(("dp", "pipe"), None),
        P("pipe", "dp", None),
        P("pipe", "dp", None),
        P("pipe", "dp", None),
        P("pipe", "dp", None),
    )
    return jax.shard_map(
        on_device, mesh=mesh, in_specs=in_specs, out_specs=out_specs, check_vma=False
    )
```

```python
import functools
import math

import jax
import jax.numpy as jnp
from jax import lax
from jax.experimental import pallas as pl
from jax.experimental.pallas import tpu as pltpu
from jax.sharding import PartitionSpec as P

HDIM = 64
NORM_EPS = 1e-05
PAIR = 2 * HDIM
VMEM_BYTES = 64 * 1024 * 1024

LONG_WORK = 11 * 10**9

F32 = jnp.float32
BF16 = jnp.bfloat16
NT = (((1,), (1,)), ((), ()))
TN = (((0,), (0,)), ((), ()))

PROJECTION_BITS = (2, 0)
OUT_BIT = 1

def dot(left, right):
    return jnp.dot(left, right, preferred_element_type=F32)


def dot_nt(left, right):
    return lax.dot_general(left, right, NT, preferred_element_type=F32)


def dot_tn(left, right):
    return lax.dot_general(left, right, TN, preferred_element_type=F32)


def call(body, name, inputs, outs, scratch=(), work=0, scalars=0, far=0, after=()):
    near = len(inputs) - scalars - far
    count = len(inputs)
    specs = [pl.BlockSpec(memory_space=pltpu.SMEM)] * scalars
    specs += [pl.BlockSpec(memory_space=pltpu.VMEM)] * near
    specs += [pl.BlockSpec(memory_space=pltpu.HBM)] * (far + len(after))

    def run(*refs):
        body(*refs[:count], *refs[count + len(after) :])

    return pl.pallas_call(
        run,
        name=name,
        out_shape=outs,
        in_specs=specs,
        out_specs=[pl.BlockSpec(memory_space=pltpu.VMEM)] * len(outs),
        scratch_shapes=list(scratch),
        compiler_params=pltpu.CompilerParams(vmem_limit_bytes=VMEM_BYTES),
        cost_estimate=pl.CostEstimate(flops=work, bytes_accessed=0, transcendentals=0),
    )(*inputs, *after)


def fetch(pairs, sems):
    copies = [
        pltpu.make_async_copy(source, target, sems.at[place])
        for place, (source, target) in enumerate(pairs)
    ]
    for copy in copies:
        copy.start()
    return copies


def finish(copies):
    for copy in copies:
        copy.wait()


def spread(bits):
    found = [0]
    for bit in bits:
        found = [index | (value << bit) for index in found for value in (0, 1)]
    return found


def groups(bits, bit_count):
    others = [bit for bit in range(bit_count) if bit not in bits]
    return [[base | part for part in spread(bits)] for base in spread(others)]


def copy_chunks(source, target, chunks, size):
    for place, chunk in enumerate(chunks):
        target[place * size : (place + 1) * size, :] = source[chunk * size : (chunk + 1) * size, :]


def bit_here(bit):
    return (lax.axis_index("dp") >> bit) & 1


def prep_body(chunks, hidden, grad, x_blocks, g_send, x, turned, sems):
    columns = g_send.shape[1]
    away = pl.ds(pl.multiple_of((1 - bit_here(OUT_BIT)) * columns, columns), columns)
    x_copy, g_copy = fetch([(hidden, x), (grad.at[:, away], g_send)], sems)
    x_copy.wait()
    turned[...] = x[...].astype(F32).T.astype(BF16)
    for member in range(4):
        own = [chunk | (member % 2) << PROJECTION_BITS[0] for chunk in chunks]
        copy_chunks(turned, x_blocks.at[member], own, turned.shape[0] // (2 * len(own)))
    g_copy.wait()


def seen_mask(pattern, seq_len, blocks, slots):
    block_len = seq_len // blocks
    rows = lax.broadcasted_iota(jnp.int32, (seq_len, seq_len), 0)
    columns = lax.broadcasted_iota(jnp.int32, (seq_len, seq_len), 1)
    row_block, column_block = rows // block_len, columns // block_len
    seen = jnp.zeros((seq_len, seq_len), F32)
    for block in range(blocks):
        for slot in range(slots):
            hit = (row_block == block) & (column_block == pattern[block, slot])
            seen = jnp.where(hit, 1.0, seen)
    return jnp.where((row_block == column_block) & (columns > rows), 0.0, seen)


def scale_of(x):
    return lax.rsqrt(jnp.mean(x * x, axis=-1, keepdims=True) + NORM_EPS)


def attention_body(
    out_chunks,
    pattern,
    x_own,
    x_mirror,
    w_query,
    w_key,
    w_value,
    g_own,
    g_mirror,
    w_out,
    attended,
    att_turned,
    blocks,
    x_all,
    weights,
    weight_out,
    g_all,
    query,
    key,
    values,
    grad_att,
    turned,
    sems,
):
    seq_len = x_own.shape[0]
    tokens = 2 * seq_len
    half = w_query.shape[1]
    own, other = pl.ds(0, seq_len), pl.ds(seq_len, seq_len)
    copies = fetch(
        [
            (x_own, x_all.at[own]),
            (x_mirror, x_all.at[other]),
            (w_query, weights.at[0]),
            (w_key, weights.at[1]),
            (w_value, weights.at[2]),
            (g_own, g_all.at[own]),
            (g_mirror, g_all.at[other]),
            (w_out, weight_out),
        ],
        sems,
    )
    finish(copies[:2])
    x = x_all[...]
    factor = scale_of(x.astype(F32))
    for place, target in enumerate((query, key, values)):
        copies[2 + place].wait()
        target[...] = (dot(x, weights[place]) * factor).astype(BF16)
    finish(copies[5:])
    grad_att[...] = dot_nt(g_all[...], weight_out[...]).astype(BF16)

    seen = seen_mask(pattern, seq_len, pattern.shape[0], pattern.shape[1])
    seen = jnp.concatenate([seen, seen], axis=0) > 0.0
    low = lax.broadcasted_iota(jnp.int32, (seq_len, PAIR), 1) < HDIM
    inv_sqrt = 1.0 / math.sqrt(HDIM)
    zero = jnp.zeros((), BF16)

    def stacked(block):
        return jnp.concatenate([jnp.where(low, block, zero), jnp.where(low, zero, block)], axis=0)

    def merged(both):
        return jnp.where(low, both[:seq_len], both[seq_len:])

    width = half // 2
    def put(member, col, first, here, value):
        rounded = value.astype(BF16)
        first += member * tokens
        for row in range(2):
            blocks[2 * col + row, first : first + seq_len, here] = rounded

    for pair in range(half // PAIR):
        columns = slice(pair * PAIR, (pair + 1) * PAIR)
        col, start = pair * PAIR // width, pair * PAIR % width
        here = slice(start, start + PAIR)
        for seq in range(2):
            rows = slice(seq * seq_len, (seq + 1) * seq_len)
            q2 = stacked(query[rows, columns])
            k = key[rows, columns]
            v = values[rows, columns]
            ga2 = stacked(grad_att[rows, columns])
            r = factor[rows]

            expo = jnp.where(seen, jnp.exp(dot_nt(q2, k) * inv_sqrt), 0.0)
            prob = expo / jnp.sum(expo, axis=-1, keepdims=True)
            prob_bf = prob.astype(BF16)
            attended[rows, columns] = merged(dot(prob_bf, v)).astype(BF16)
            grad_prob = dot_nt(ga2, v)
            inner = jnp.sum(prob * grad_prob, axis=-1, keepdims=True)
            score = (prob * (grad_prob - inner) * inv_sqrt).astype(BF16)
            put(0, col, seq * seq_len, here, dot_tn(prob_bf, ga2) * r)
            put(1, col, seq * seq_len, here, dot_tn(score, q2) * r)
            put(2, col, seq * seq_len, here, merged(dot(score, k)) * r)

    turned[...] = attended[...].astype(F32).T.astype(BF16)
    copy_chunks(turned, att_turned, out_chunks, half // len(out_chunks))


def returned_body(
    x_own,
    x_mirror,
    attended,
    w_out,
    w_query,
    w_key,
    w_value,
    blocks,
    contrib_own,
    contrib_mirror,
    returned_own,
    returned_mirror,
    x_all,
    att,
    weight_out,
    weights,
    grads,
    sems,
):
    seq_len = x_own.shape[0]
    tokens, half = att.shape
    width = half // 2
    pairs = [
        (attended, att),
        (w_out, weight_out),
        (x_own, x_all.at[pl.ds(0, seq_len)]),
        (x_mirror, x_all.at[pl.ds(seq_len, seq_len)]),
    ]
    for member in range(3):
        for col in range(2):
            source = blocks.at[2 * col, pl.ds(member * tokens, tokens)]
            pairs.append((source, grads.at[member, :, pl.ds(col * width, width)]))
    pairs += [(w_value, weights.at[0]), (w_key, weights.at[1]), (w_query, weights.at[2])]
    copies = fetch(pairs, sems)
    finish(copies[:2])
    contrib = dot(att[...], weight_out[...]).astype(BF16)
    contrib_own[...] = contrib[:seq_len]
    contrib_mirror[...] = contrib[seq_len:]
    finish(copies[2:-3])
    grad = None
    for member in range(3):
        copies[member - 3].wait()
        term = dot_nt(grads[member], weights[member])
        grad = term if grad is None else grad + term
    x = x_all[...].astype(F32)
    factor = scale_of(x)
    mean_term = jnp.mean(x * grad, axis=-1, keepdims=True)
    returned = (grad - x * (factor * factor * mean_term)).astype(BF16)
    returned_own[...] = returned[:seq_len]
    returned_mirror[...] = returned[seq_len:]


def projection_grad_body(bits, x_pieces, x_mirrors, g_pieces, *rest):
    pair_send, pair_keep, query_send, query_keep, x_all, right, sems = rest
    seq_len = x_pieces.shape[2]
    tokens = 2 * seq_len
    width = g_pieces.shape[2]
    pairs = []
    for place in range(4):
        for at, source in enumerate((x_pieces, x_mirrors)):
            columns = pl.ds(place * tokens + at * seq_len, seq_len)
            pairs.append((source.at[place], x_all.at[:, columns]))
        for member in range(3):
            target = right.at[pl.ds(place * tokens, tokens), pl.ds(member * width, width)]
            pairs.append((g_pieces.at[place, pl.ds(member * tokens, tokens)], target))
    finish(fetch(pairs, sems))
    rows = x_all.shape[0] // 2
    bit = bit_here(bits[0])
    for target, side in ((pair_send, 1 - bit), (pair_keep, bit)):
        part = pl.ds(pl.multiple_of(side * rows, rows), rows)
        target[...] = dot(x_all[part, :], right[:, : 2 * width]).astype(BF16)
    bit = bit_here(bits[1])
    for target, side in ((query_send, 1 - bit), (query_keep, bit)):
        for turn in range(2):
            start = pl.multiple_of(turn * rows + side * (rows // 2), rows // 2)
            grad = dot(x_all[pl.ds(start, rows // 2), :], right[:, 2 * width :]).astype(BF16)
            target[turn * (rows // 2) : (turn + 1) * (rows // 2), :] = grad


def out_grad_body(bits, grad, g_mirror, g_piece, g_piece_mirror, att_own, att_piece, *rest):
    targets, (left, right, sems) = rest[:4], rest[4:]
    seq_len = grad.shape[0]
    tokens = 2 * seq_len
    columns = right.shape[1]
    here = pl.ds(pl.multiple_of(bit_here(OUT_BIT) * columns, columns), columns)
    pairs = [
        (att_own, left.at[:, pl.ds(0, tokens)]),
        (att_piece, left.at[:, pl.ds(tokens, tokens)]),
    ]
    for place, source in enumerate(
        (grad.at[:, here], g_mirror.at[:, here], g_piece, g_piece_mirror)
    ):
        pairs.append((source, right.at[pl.ds(place * seq_len, seq_len)]))
    finish(fetch(pairs, sems))
    own = 2 * bit_here(bits[0]) + bit_here(bits[1])
    rows = left.shape[0] // 4
    for place, target in enumerate(targets):
        part = pl.ds(pl.multiple_of((own ^ place) * rows, rows), rows)
        target[...] = dot(left[part, :], right[...]).astype(BF16)


def halve_body(bit, count, *refs):
    sources, (send, keep, sides, sems) = refs[:count], refs[count:]
    here = bit_here(bit)
    rows = send.shape[0]
    pairs = []
    for turn, side in ((0, 1 - here), (1, here)):
        part = pl.ds(pl.multiple_of(side * rows, rows), rows)
        pairs += [(ref.at[part], sides.at[turn, at]) for at, ref in enumerate(sources)]
    copies = fetch(pairs, sems)
    for turn, target in ((0, send), (1, keep)):
        finish(copies[turn * count : (turn + 1) * count])
        total = sides[turn, 0].astype(F32)
        for at in range(1, count):
            total += sides[turn, at].astype(F32)
        target[...] = total.astype(BF16)


def out_final_body(keep, other, target):
    columns = keep.shape[1]
    here = bit_here(OUT_BIT)
    for source, col in ((keep, here), (other, 1 - here)):
        target[:, pl.ds(pl.multiple_of(col * columns, columns), columns)] = source[...].astype(F32)


def final_body(pieces, query_keep, query_other, *targets):
    columns = targets[0].shape[1] // 2
    for col in range(2):
        total = pieces[col].astype(F32)
        for place in range(1, pieces.shape[0] // 2):
            total += pieces[2 * place + col].astype(F32)
        for member in range(2):
            targets[member][:, col * columns : (col + 1) * columns] = total[
                :, member * columns : (member + 1) * columns
            ]
    here = bit_here(PROJECTION_BITS[1])
    for source, col in ((query_keep, here), (query_other, 1 - here)):
        place = pl.ds(pl.multiple_of(col * columns, columns), columns)
        targets[2][:, place] = source[...].astype(F32)


def on_device(hidden_in, grad_out, w_query, w_key, w_value, w_out, pattern):
    replicas = lax.axis_size("dp")
    pipe = lax.axis_size("pipe")
    bit_count = replicas.bit_length() - 1
    row_bit, col_bit = PROJECTION_BITS
    halved_bits = [bit for bit in range(bit_count) if bit not in PROJECTION_BITS]
    out_bits = [col_bit, row_bit] + [bit for bit in halved_bits if bit != OUT_BIT]
    chunks = spread(halved_bits + [col_bit])
    out_chunks = spread(out_bits + [OUT_BIT])
    seq_len, features = hidden_in.shape
    half = w_query.shape[2]
    w_query, w_key, w_value, w_out = w_query[0], w_key[0], w_value[0], w_out[0]
    width, part, tokens = half // 2, features // 2, 2 * seq_len

    def swap(x, *bits):
        apart = sum(1 << bit for bit in bits)
        return lax.ppermute(x, "dp", [(i, i ^ apart) for i in range(replicas)])

    def mirror(x):
        return lax.ppermute(x, "pipe", [(i, pipe - 1 - i) for i in range(pipe)])

    def exchange(x, bits):
        members = groups(bits, bit_count)
        return lax.all_to_all(x, "dp", 0, 0, axis_index_groups=members, tiled=True)

    def follows(x, before):
        return lax.optimization_barrier((x, before))[0]

    def bf16(*shape):
        return jax.ShapeDtypeStruct(shape, BF16)

    x_mirror = mirror(hidden_in)
    g_mirror = mirror(grad_out)
    x_blocks, g_send = call(
        functools.partial(prep_body, chunks),
        "prep",
        (hidden_in, grad_out),
        [bf16(4, part, seq_len), bf16(seq_len, part)],
        [
            pltpu.VMEM((seq_len, features), BF16),
            pltpu.VMEM((features, seq_len), BF16),
            pltpu.SemaphoreType.DMA((2,)),
        ],
        far=2,
    )
    x_pieces = exchange(x_blocks, [col_bit, row_bit])
    g_piece = swap(g_send, OUT_BIT)

    attended, att_turned, g_blocks = call(
        functools.partial(attention_body, out_chunks),
        "attention",
        (pattern, hidden_in, x_mirror, w_query, w_key, w_value, grad_out, g_mirror, w_out),
        [bf16(tokens, half), bf16(half, tokens)]
        + [bf16(4, 3 * tokens, width)],
        [
            pltpu.VMEM((tokens, features), BF16),
            pltpu.VMEM((3, features, half), BF16),
            pltpu.VMEM((half, features), BF16),
            pltpu.VMEM((tokens, features), BF16),
        ]
        + [pltpu.VMEM((tokens, half), BF16)] * 4
        + [
            pltpu.VMEM((half, tokens), BF16),
            pltpu.SemaphoreType.DMA((8,)),
        ],
        work=LONG_WORK,
        scalars=1,
        far=8,
        after=(x_blocks,),
    )
    g_pieces = exchange(follows(g_blocks, g_piece), [col_bit, row_bit])
    att_piece = swap(att_turned, OUT_BIT)
    x_mirrors = mirror(follows(x_pieces, attended))
    g_piece_mirror = mirror(follows(g_piece, attended))

    contrib, contrib_mirror, returned, returned_mirror = call(
        returned_body,
        "returned",
        (hidden_in, x_mirror, attended, w_out, w_query, w_key, w_value, g_blocks),
        [bf16(seq_len, features)] * 4,
        [
            pltpu.VMEM((tokens, features), BF16),
            pltpu.VMEM((tokens, half), BF16),
            pltpu.VMEM((half, features), BF16),
            pltpu.VMEM((3, features, half), BF16),
            pltpu.VMEM((3, tokens, half), BF16),
            pltpu.SemaphoreType.DMA((13,)),
        ],
        far=8,
    )

    out_keep, *out_sends = call(
        functools.partial(out_grad_body, out_bits[:2]),
        "out_grad",
        (grad_out, g_mirror, g_piece, g_piece_mirror, att_turned, att_piece),
        [bf16(half // 4, part)] * 4,
        [
            pltpu.VMEM((half, 2 * tokens), BF16),
            pltpu.VMEM((2 * tokens, part), BF16),
            pltpu.SemaphoreType.DMA((6,)),
        ],
        far=6,
        after=(contrib, x_mirrors),
    )
    out_arrived = [
        swap(out_sends[0], out_bits[1]),
        swap(out_sends[1], out_bits[0]),
        swap(out_sends[2], *out_bits[:2]),
    ]
    pair_send, pair_keep, query_send, query_keep = call(
        functools.partial(projection_grad_body, halved_bits),
        "projection_grad",
        (x_pieces, x_mirrors, g_pieces),
        [bf16(part // 2, 2 * width)] * 2 + [bf16(part // 2, width)] * 2,
        [
            pltpu.VMEM((part, 4 * tokens), BF16),
            pltpu.VMEM((4 * tokens, 3 * width), BF16),
            pltpu.SemaphoreType.DMA((20,)),
        ],
        far=3,
        after=(out_keep,),
    )
    pair_arrived = swap(pair_send, halved_bits[0])
    query_arrived = swap(query_send, halved_bits[1])

    def halve(arrays, next_bit, after, work=0):
        count, shape = len(arrays), (arrays[0].shape[0] // 2, arrays[0].shape[1])
        return call(
            functools.partial(halve_body, next_bit, count),
            "halve",
            arrays,
            [bf16(*shape)] * 2,
            [pltpu.VMEM((2, count, *shape), BF16), pltpu.SemaphoreType.DMA((2 * count,))],
            work=work,
            far=count,
            after=(after,),
        )

    def stepped(arrays, bits, after, work=0):
        send, keep = halve(arrays, bits[0], after, work)
        return [keep, swap(send, bits[0])], bits[1:], send

    out, out_left, last = stepped(
        [out_keep] + out_arrived, out_bits[2:] + [OUT_BIT], pair_send, LONG_WORK
    )
    contrib_other = mirror(follows(contrib_mirror, last))
    returned_other = mirror(follows(returned_mirror, last))
    hidden_out = (
        hidden_in.astype(F32) + contrib.astype(F32) + contrib_other.astype(F32)
    ).astype(BF16)
    grad_in = (
        grad_out.astype(F32) + returned.astype(F32) + returned_other.astype(F32)
    ).astype(BF16)

    pair_total = pair_keep.astype(F32) + follows(pair_arrived, (last, query_arrived)).astype(F32)
    pair_total = pair_total.astype(BF16)
    pieces = exchange(pair_total, halved_bits[1:] + [col_bit])
    query, query_left = [query_keep, query_arrived], [halved_bits[0]] + halved_bits[2:] + [col_bit]
    last = pair_total
    while query_left or out_left:
        if query_left:
            query, query_left, last = stepped(query, query_left, last)
        if out_left:
            out, out_left, last = stepped(out, out_left, last)
    (grad_wout,) = call(
        out_final_body,
        "out_final",
        out,
        [jax.ShapeDtypeStruct((half // replicas, features), F32)],
        after=(last,),
    )
    grads = call(
        final_body,
        "final",
        (pieces.reshape(1 << len(halved_bits), -1, 2 * width), *query),
        [jax.ShapeDtypeStruct((features // replicas, half), F32)] * 3,
        after=(grad_wout,),
    )
    grad_value, grad_key, grad_query = (grad[None] for grad in grads)
    return (hidden_out, grad_in, grad_query, grad_key, grad_value, grad_wout[None])


def solution(mesh):
    in_specs = (
        P(("dp", "pipe"), None),
        P(("dp", "pipe"), None),
        P("pipe", None, None),
        P("pipe", None, None),
        P("pipe", None, None),
        P("pipe", None, None),
        P(),
    )
    out_specs = (
        P(("dp", "pipe"), None),
        P(("dp", "pipe"), None),
        P("pipe", "dp", None),
        P("pipe", "dp", None),
        P("pipe", "dp", None),
        P("pipe", "dp", None),
    )
    return jax.shard_map(
        on_device, mesh=mesh, in_specs=in_specs, out_specs=out_specs, check_vma=False
    )
```

```python
import functools
import math

import jax
import jax.numpy as jnp
from jax import lax
from jax.experimental import pallas as pl
from jax.experimental.pallas import tpu as pltpu
from jax.sharding import PartitionSpec as P

HDIM = 64
NORM_EPS = 1e-05
PAIR = 2 * HDIM
VMEM_BYTES = 64 * 1024 * 1024

LONG_WORK = 11 * 10**9

F32 = jnp.float32
BF16 = jnp.bfloat16
NT = (((1,), (1,)), ((), ()))
TN = (((0,), (0,)), ((), ()))

PROJECTION_BITS = (2, 0)
OUT_BIT = 1

def dot(left, right):
    return jnp.dot(left, right, preferred_element_type=F32)


def dot_nt(left, right):
    return lax.dot_general(left, right, NT, preferred_element_type=F32)


def dot_tn(left, right):
    return lax.dot_general(left, right, TN, preferred_element_type=F32)


def call(body, name, inputs, outs, scratch=(), work=0, scalars=0, far=0, after=()):
    near = len(inputs) - scalars - far
    count = len(inputs)
    specs = [pl.BlockSpec(memory_space=pltpu.SMEM)] * scalars
    specs += [pl.BlockSpec(memory_space=pltpu.VMEM)] * near
    specs += [pl.BlockSpec(memory_space=pltpu.HBM)] * (far + len(after))

    def run(*refs):
        body(*refs[:count], *refs[count + len(after) :])

    return pl.pallas_call(
        run,
        name=name,
        out_shape=outs,
        in_specs=specs,
        out_specs=[pl.BlockSpec(memory_space=pltpu.VMEM)] * len(outs),
        scratch_shapes=list(scratch),
        compiler_params=pltpu.CompilerParams(vmem_limit_bytes=VMEM_BYTES),
        cost_estimate=pl.CostEstimate(flops=work, bytes_accessed=0, transcendentals=0),
    )(*inputs, *after)


def fetch(pairs, sems):
    copies = [
        pltpu.make_async_copy(source, target, sems.at[place])
        for place, (source, target) in enumerate(pairs)
    ]
    for copy in copies:
        copy.start()
    return copies


def finish(copies):
    for copy in copies:
        copy.wait()


def spread(bits):
    found = [0]
    for bit in bits:
        found = [index | (value << bit) for index in found for value in (0, 1)]
    return found


def groups(bits, bit_count):
    others = [bit for bit in range(bit_count) if bit not in bits]
    return [[base | part for part in spread(bits)] for base in spread(others)]


def copy_chunks(source, target, chunks, size):
    for place, chunk in enumerate(chunks):
        target[place * size : (place + 1) * size, :] = source[chunk * size : (chunk + 1) * size, :]


def bit_here(bit):
    return (lax.axis_index("dp") >> bit) & 1


def prep_body(chunks, hidden, grad, x_blocks, g_send, x, turned, sems):
    columns = g_send.shape[1]
    away = pl.ds(pl.multiple_of((1 - bit_here(OUT_BIT)) * columns, columns), columns)
    x_copy, g_copy = fetch([(hidden, x), (grad.at[:, away], g_send)], sems)
    x_copy.wait()
    turned[...] = x[...].astype(F32).T.astype(BF16)
    for member in range(4):
        own = [chunk | (member % 2) << PROJECTION_BITS[0] for chunk in chunks]
        copy_chunks(turned, x_blocks.at[member], own, turned.shape[0] // (2 * len(own)))
    g_copy.wait()


def seen_mask(pattern, seq_len, blocks, slots):
    block_len = seq_len // blocks
    rows = lax.broadcasted_iota(jnp.int32, (seq_len, seq_len), 0)
    columns = lax.broadcasted_iota(jnp.int32, (seq_len, seq_len), 1)
    row_block, column_block = rows // block_len, columns // block_len
    seen = jnp.zeros((seq_len, seq_len), F32)
    for block in range(blocks):
        for slot in range(slots):
            hit = (row_block == block) & (column_block == pattern[block, slot])
            seen = jnp.where(hit, 1.0, seen)
    return jnp.where((row_block == column_block) & (columns > rows), 0.0, seen)


def scale_of(x):
    return lax.rsqrt(jnp.mean(x * x, axis=-1, keepdims=True) + NORM_EPS)


def attention_body(
    out_chunks,
    pattern,
    x_own,
    x_mirror,
    w_query,
    w_key,
    w_value,
    g_own,
    g_mirror,
    w_out,
    attended,
    att_turned,
    blocks,
    x_all,
    weights,
    weight_out,
    g_all,
    query,
    key,
    values,
    grad_att,
    turned,
    sems,
):
    seq_len = x_own.shape[0]
    tokens = 2 * seq_len
    half = w_query.shape[1]
    own, other = pl.ds(0, seq_len), pl.ds(seq_len, seq_len)
    copies = fetch(
        [
            (x_own, x_all.at[own]),
            (x_mirror, x_all.at[other]),
            (w_query, weights.at[0]),
            (w_key, weights.at[1]),
            (w_value, weights.at[2]),
            (g_own, g_all.at[own]),
            (g_mirror, g_all.at[other]),
            (w_out, weight_out),
        ],
        sems,
    )
    finish(copies[:2])
    x = x_all[...]
    factor = scale_of(x.astype(F32))
    for place, target in enumerate((query, key, values)):
        copies[2 + place].wait()
        target[...] = (dot(x, weights[place]) * factor).astype(BF16)
    finish(copies[5:])
    grad_att[...] = dot_nt(g_all[...], weight_out[...]).astype(BF16)

    seen = seen_mask(pattern, seq_len, pattern.shape[0], pattern.shape[1])
    seen = jnp.concatenate([seen, seen], axis=0) > 0.0
    low = lax.broadcasted_iota(jnp.int32, (seq_len, PAIR), 1) < HDIM
    inv_sqrt = 1.0 / math.sqrt(HDIM)
    zero = jnp.zeros((), BF16)

    def stacked(block):
        return jnp.concatenate([jnp.where(low, block, zero), jnp.where(low, zero, block)], axis=0)

    def merged(both):
        return jnp.where(low, both[:seq_len], both[seq_len:])

    width = half // 2
    def put(member, col, first, here, value):
        rounded = value.astype(BF16)
        first += member * tokens
        for row in range(2):
            blocks[2 * col + row, first : first + seq_len, here] = rounded

    for pair in range(half // PAIR):
        columns = slice(pair * PAIR, (pair + 1) * PAIR)
        col, start = pair * PAIR // width, pair * PAIR % width
        here = slice(start, start + PAIR)
        for seq in range(2):
            rows = slice(seq * seq_len, (seq + 1) * seq_len)
            q2 = stacked(query[rows, columns])
            k = key[rows, columns]
            v = values[rows, columns]
            ga2 = stacked(grad_att[rows, columns])
            r = factor[rows]

            expo = jnp.where(seen, jnp.exp(dot_nt(q2, k) * inv_sqrt), 0.0)
            prob = expo / jnp.sum(expo, axis=-1, keepdims=True)
            prob_bf = prob.astype(BF16)
            attended[rows, columns] = merged(dot(prob_bf, v)).astype(BF16)
            grad_prob = dot_nt(ga2, v)
            inner = jnp.sum(prob * grad_prob, axis=-1, keepdims=True)
            score = (prob * (grad_prob - inner) * inv_sqrt).astype(BF16)
            put(0, col, seq * seq_len, here, dot_tn(prob_bf, ga2) * r)
            put(1, col, seq * seq_len, here, dot_tn(score, q2) * r)
            put(2, col, seq * seq_len, here, merged(dot(score, k)) * r)

    turned[...] = attended[...].astype(F32).T.astype(BF16)
    copy_chunks(turned, att_turned, out_chunks, half // len(out_chunks))


def returned_body(
    x_own,
    x_mirror,
    attended,
    w_out,
    w_query,
    w_key,
    w_value,
    blocks,
    contrib_own,
    contrib_mirror,
    returned_own,
    returned_mirror,
    x_all,
    att,
    weight_out,
    weights,
    grads,
    sems,
):
    seq_len = x_own.shape[0]
    tokens, half = att.shape
    width = half // 2
    pairs = [
        (attended, att),
        (w_out, weight_out),
        (x_own, x_all.at[pl.ds(0, seq_len)]),
        (x_mirror, x_all.at[pl.ds(seq_len, seq_len)]),
    ]
    for member in range(3):
        for col in range(2):
            source = blocks.at[2 * col, pl.ds(member * tokens, tokens)]
            pairs.append((source, grads.at[member, :, pl.ds(col * width, width)]))
    pairs += [(w_value, weights.at[0]), (w_key, weights.at[1]), (w_query, weights.at[2])]
    copies = fetch(pairs, sems)
    finish(copies[:2])
    contrib = dot(att[...], weight_out[...]).astype(BF16)
    contrib_own[...] = contrib[:seq_len]
    contrib_mirror[...] = contrib[seq_len:]
    finish(copies[2:-3])
    grad = None
    for member in range(3):
        copies[member - 3].wait()
        term = dot_nt(grads[member], weights[member])
        grad = term if grad is None else grad + term
    x = x_all[...].astype(F32)
    factor = scale_of(x)
    mean_term = jnp.mean(x * grad, axis=-1, keepdims=True)
    returned = (grad - x * (factor * factor * mean_term)).astype(BF16)
    returned_own[...] = returned[:seq_len]
    returned_mirror[...] = returned[seq_len:]


def projection_grad_body(bits, x_pieces, x_mirrors, g_pieces, *rest):
    pair_send, pair_keep, query_send, query_keep, x_all, right, sems = rest
    seq_len = x_pieces.shape[2]
    tokens = 2 * seq_len
    width = g_pieces.shape[2]
    pairs = []
    for place in range(4):
        for at, source in enumerate((x_pieces, x_mirrors)):
            columns = pl.ds(place * tokens + at * seq_len, seq_len)
            pairs.append((source.at[place], x_all.at[:, columns]))
        for member in range(3):
            target = right.at[pl.ds(place * tokens, tokens), pl.ds(member * width, width)]
            pairs.append((g_pieces.at[place, pl.ds(member * tokens, tokens)], target))
    finish(fetch(pairs, sems))
    rows = x_all.shape[0] // 2
    bit = bit_here(bits[0])
    for target, side in ((pair_send, 1 - bit), (pair_keep, bit)):
        part = pl.ds(pl.multiple_of(side * rows, rows), rows)
        target[...] = dot(x_all[part, :], right[:, : 2 * width]).astype(BF16)
    bit = bit_here(bits[1])
    count = 1 << (len(bits) - 2)
    size = rows // 2 // count
    for target, side in ((query_send, 1 - bit), (query_keep, bit)):
        for turn in range(2):
            for place in range(count):
                start = turn * rows + side * (rows // 2) + place * size
                part = pl.ds(pl.multiple_of(start, size), size)
                grad = dot(x_all[part, :], right[:, 2 * width :]).astype(BF16)
                first = (2 * place + turn) * size
                target[first : first + size, :] = grad


def out_grad_body(bits, grad, g_mirror, g_piece, g_piece_mirror, att_own, att_piece, *rest):
    targets, (left, right, sems) = rest[:4], rest[4:]
    seq_len = grad.shape[0]
    tokens = 2 * seq_len
    columns = right.shape[1]
    here = pl.ds(pl.multiple_of(bit_here(OUT_BIT) * columns, columns), columns)
    pairs = [
        (att_own, left.at[:, pl.ds(0, tokens)]),
        (att_piece, left.at[:, pl.ds(tokens, tokens)]),
    ]
    for place, source in enumerate(
        (grad.at[:, here], g_mirror.at[:, here], g_piece, g_piece_mirror)
    ):
        pairs.append((source, right.at[pl.ds(place * seq_len, seq_len)]))
    finish(fetch(pairs, sems))
    own = 2 * bit_here(bits[0]) + bit_here(bits[1])
    rows = left.shape[0] // 4
    for place, target in enumerate(targets):
        part = pl.ds(pl.multiple_of((own ^ place) * rows, rows), rows)
        target[...] = dot(left[part, :], right[...]).astype(BF16)


def halve_body(bit, count, *refs):
    sources, (send, keep, sides, sems) = refs[:count], refs[count:]
    here = bit_here(bit)
    rows = send.shape[0]
    pairs = []
    for turn, side in ((0, 1 - here), (1, here)):
        part = pl.ds(pl.multiple_of(side * rows, rows), rows)
        pairs += [(ref.at[part], sides.at[turn, at]) for at, ref in enumerate(sources)]
    copies = fetch(pairs, sems)
    for turn, target in ((0, send), (1, keep)):
        finish(copies[turn * count : (turn + 1) * count])
        total = sides[turn, 0].astype(F32)
        for at in range(1, count):
            total += sides[turn, at].astype(F32)
        target[...] = total.astype(BF16)


def meet_body(
    col_bit, query_keep, query_arrived, out_keep, out_arrived, own, send_out, send_col, send_both, *rest
):
    next_out, query, out, sems = rest
    here = bit_here(OUT_BIT)
    col = bit_here(col_bit)
    rows, out_rows, width = own.shape[0], next_out.shape[0], own.shape[1]
    copies = fetch(
        [
            (query_keep, query.at[0]),
            (query_arrived, query.at[1]),
            (out_keep, out.at[0]),
            (out_arrived, out.at[1]),
        ],
        sems,
    )

    def total(both, block, extent):
        part = pl.ds(pl.multiple_of(block * extent, extent), extent)
        return (both[0, part, :].astype(F32) + both[1, part, :].astype(F32)).astype(BF16)

    finish(copies[:2])
    own[...] = total(query, 2 * here + col, rows)
    send_out[:rows, :] = total(query, 2 * (1 - here) + col, rows)
    send_col[...] = total(query, 2 * here + 1 - col, rows)
    send_both[...] = total(query, 2 * (1 - here) + 1 - col, rows)
    finish(copies[2:])
    away = total(out, 1 - here, out_rows)
    for place in range(next_out.shape[1] // width):
        first = rows + place * out_rows
        send_out[first : first + out_rows, :] = away[:, place * width : (place + 1) * width]
    next_out[...] = total(out, here, out_rows)


def final_body(pieces, own, from_out, from_col, from_both, out_own, *targets):
    columns = targets[0].shape[1] // 2
    for col in range(2):
        total = pieces[col].astype(F32)
        for place in range(1, pieces.shape[0] // 2):
            total += pieces[2 * place + col].astype(F32)
        for member in range(2):
            targets[member][:, col * columns : (col + 1) * columns] = total[
                :, member * columns : (member + 1) * columns
            ]
    here = bit_here(PROJECTION_BITS[1])
    rows = own.shape[0]
    for one, two, col in ((own, from_out, here), (from_col, from_both, 1 - here)):
        place = pl.ds(pl.multiple_of(col * columns, columns), columns)
        targets[2][:, place] = one[...].astype(F32) + two[:rows, :].astype(F32)
    here = bit_here(OUT_BIT)
    out_rows, out_columns = out_own.shape
    place = pl.ds(pl.multiple_of(here * out_columns, out_columns), out_columns)
    targets[3][:, place] = out_own[...].astype(F32)
    for at in range(out_columns // columns):
        start = (1 - here) * out_columns + at * columns
        first = rows + at * out_rows
        block = from_out[first : first + out_rows, :].astype(F32)
        targets[3][:, pl.ds(pl.multiple_of(start, columns), columns)] = block


def on_device(hidden_in, grad_out, w_query, w_key, w_value, w_out, pattern):
    replicas = lax.axis_size("dp")
    pipe = lax.axis_size("pipe")
    bit_count = replicas.bit_length() - 1
    row_bit, col_bit = PROJECTION_BITS
    halved_bits = [bit for bit in range(bit_count) if bit not in PROJECTION_BITS]
    out_bits = [col_bit, row_bit] + [bit for bit in halved_bits if bit != OUT_BIT]
    chunks = spread(halved_bits + [col_bit])
    out_chunks = spread(out_bits + [OUT_BIT])
    seq_len, features = hidden_in.shape
    half = w_query.shape[2]
    w_query, w_key, w_value, w_out = w_query[0], w_key[0], w_value[0], w_out[0]
    width, part, tokens = half // 2, features // 2, 2 * seq_len

    def swap(x, *bits):
        apart = sum(1 << bit for bit in bits)
        return lax.ppermute(x, "dp", [(i, i ^ apart) for i in range(replicas)])

    def mirror(x):
        return lax.ppermute(x, "pipe", [(i, pipe - 1 - i) for i in range(pipe)])

    def exchange(x, bits):
        members = groups(bits, bit_count)
        return lax.all_to_all(x, "dp", 0, 0, axis_index_groups=members, tiled=True)

    def follows(x, before):
        return lax.optimization_barrier((x, before))[0]

    def bf16(*shape):
        return jax.ShapeDtypeStruct(shape, BF16)

    x_mirror = mirror(hidden_in)
    g_mirror = mirror(grad_out)
    x_blocks, g_send = call(
        functools.partial(prep_body, chunks),
        "prep",
        (hidden_in, grad_out),
        [bf16(4, part, seq_len), bf16(seq_len, part)],
        [
            pltpu.VMEM((seq_len, features), BF16),
            pltpu.VMEM((features, seq_len), BF16),
            pltpu.SemaphoreType.DMA((2,)),
        ],
        far=2,
    )
    x_pieces = exchange(x_blocks, [col_bit, row_bit])
    g_piece = swap(g_send, OUT_BIT)

    attended, att_turned, g_blocks = call(
        functools.partial(attention_body, out_chunks),
        "attention",
        (pattern, hidden_in, x_mirror, w_query, w_key, w_value, grad_out, g_mirror, w_out),
        [bf16(tokens, half), bf16(half, tokens)]
        + [bf16(4, 3 * tokens, width)],
        [
            pltpu.VMEM((tokens, features), BF16),
            pltpu.VMEM((3, features, half), BF16),
            pltpu.VMEM((half, features), BF16),
            pltpu.VMEM((tokens, features), BF16),
        ]
        + [pltpu.VMEM((tokens, half), BF16)] * 4
        + [
            pltpu.VMEM((half, tokens), BF16),
            pltpu.SemaphoreType.DMA((8,)),
        ],
        work=LONG_WORK,
        scalars=1,
        far=8,
        after=(x_blocks,),
    )
    g_pieces = exchange(follows(g_blocks, g_piece), [col_bit, row_bit])
    att_piece = swap(att_turned, OUT_BIT)
    x_mirrors = mirror(follows(x_pieces, attended))
    g_piece_mirror = mirror(follows(g_piece, attended))

    contrib, contrib_mirror, returned, returned_mirror = call(
        returned_body,
        "returned",
        (hidden_in, x_mirror, attended, w_out, w_query, w_key, w_value, g_blocks),
        [bf16(seq_len, features)] * 4,
        [
            pltpu.VMEM((tokens, features), BF16),
            pltpu.VMEM((tokens, half), BF16),
            pltpu.VMEM((half, features), BF16),
            pltpu.VMEM((3, features, half), BF16),
            pltpu.VMEM((3, tokens, half), BF16),
            pltpu.SemaphoreType.DMA((13,)),
        ],
        far=8,
    )

    out_keep, *out_sends = call(
        functools.partial(out_grad_body, out_bits[:2]),
        "out_grad",
        (grad_out, g_mirror, g_piece, g_piece_mirror, att_turned, att_piece),
        [bf16(half // 4, part)] * 4,
        [
            pltpu.VMEM((half, 2 * tokens), BF16),
            pltpu.VMEM((2 * tokens, part), BF16),
            pltpu.SemaphoreType.DMA((6,)),
        ],
        far=6,
        after=(contrib, x_mirrors),
    )
    out_arrived = [
        swap(out_sends[0], out_bits[1]),
        swap(out_sends[1], out_bits[0]),
        swap(out_sends[2], *out_bits[:2]),
    ]
    pair_send, pair_keep, query_send, query_keep = call(
        functools.partial(projection_grad_body, halved_bits),
        "projection_grad",
        (x_pieces, x_mirrors, g_pieces),
        [bf16(part // 2, 2 * width)] * 2 + [bf16(part // 2, width)] * 2,
        [
            pltpu.VMEM((part, 4 * tokens), BF16),
            pltpu.VMEM((4 * tokens, 3 * width), BF16),
            pltpu.SemaphoreType.DMA((20,)),
        ],
        far=3,
        after=(out_keep,),
    )
    pair_arrived = swap(pair_send, halved_bits[0])
    query_arrived = swap(query_send, halved_bits[1])

    def halve(arrays, next_bit, after, work=0):
        count, shape = len(arrays), (arrays[0].shape[0] // 2, arrays[0].shape[1])
        return call(
            functools.partial(halve_body, next_bit, count),
            "halve",
            arrays,
            [bf16(*shape)] * 2,
            [pltpu.VMEM((2, count, *shape), BF16), pltpu.SemaphoreType.DMA((2 * count,))],
            work=work,
            far=count,
            after=(after,),
        )

    def stepped(arrays, bits, after, work=0):
        send, keep = halve(arrays, bits[0], after, work)
        return [keep, swap(send, bits[0])], bits[1:], send

    out, out_left, last = stepped(
        [out_keep] + out_arrived, out_bits[2:] + [OUT_BIT], pair_send, LONG_WORK
    )
    contrib_other = mirror(follows(contrib_mirror, last))
    returned_other = mirror(follows(returned_mirror, last))
    hidden_out = (
        hidden_in.astype(F32) + contrib.astype(F32) + contrib_other.astype(F32)
    ).astype(BF16)
    grad_in = (
        grad_out.astype(F32) + returned.astype(F32) + returned_other.astype(F32)
    ).astype(BF16)

    pair_total = pair_keep.astype(F32) + follows(pair_arrived, (last, query_arrived)).astype(F32)
    pair_total = pair_total.astype(BF16)
    pieces = exchange(pair_total, halved_bits[1:] + [col_bit])
    last = pair_total
    while out_left[1:]:
        out, out_left, last = stepped(out, out_left, last)
    query = [query_keep, query_arrived]
    for bit in halved_bits[2:]:
        query, _, last = stepped(query, [bit], last)
    rows, out_rows = features // replicas, half // replicas
    own, send_out, send_col, send_both, out_own = call(
        functools.partial(meet_body, col_bit),
        "meet",
        (*query, *out),
        [bf16(rows, width), bf16(rows + out_rows * (part // width), width)]
        + [bf16(rows, width)] * 2
        + [bf16(out_rows, part)],
        [
            pltpu.VMEM((2, 4 * rows, width), BF16),
            pltpu.VMEM((2, 2 * out_rows, part), BF16),
            pltpu.SemaphoreType.DMA((4,)),
        ],
        far=4,
        after=(last,),
    )
    blocks = [
        own,
        swap(send_out, OUT_BIT),
        swap(send_col, col_bit),
        swap(send_both, OUT_BIT, col_bit),
        out_own,
    ]
    grads = call(
        final_body,
        "final",
        (pieces.reshape(1 << len(halved_bits), -1, 2 * width), *blocks),
        [jax.ShapeDtypeStruct((rows, half), F32)] * 3
        + [jax.ShapeDtypeStruct((out_rows, features), F32)],
    )
    grad_value, grad_key, grad_query, grad_wout = (grad[None] for grad in grads)
    return (hidden_out, grad_in, grad_query, grad_key, grad_value, grad_wout)


def solution(mesh):
    in_specs = (
        P(("dp", "pipe"), None),
        P(("dp", "pipe"), None),
        P("pipe", None, None),
        P("pipe", None, None),
        P("pipe", None, None),
        P("pipe", None, None),
        P(),
    )
    out_specs = (
        P(("dp", "pipe"), None),
        P(("dp", "pipe"), None),
        P("pipe", "dp", None),
        P("pipe", "dp", None),
        P("pipe", "dp", None),
        P("pipe", "dp", None),
    )
    return jax.shard_map(
        on_device, mesh=mesh, in_specs=in_specs, out_specs=out_specs, check_vma=False
    )
```

```python
import functools
import math

import jax
import jax.numpy as jnp
from jax import lax
from jax.experimental import pallas as pl
from jax.experimental.pallas import tpu as pltpu
from jax.sharding import PartitionSpec as P

HDIM = 64
NORM_EPS = 1e-05
PAIR = 2 * HDIM
VMEM_BYTES = 64 * 1024 * 1024

LATE_VMEM_BYTES = 16 * 1024 * 1024

LONG_WORK = 11 * 10**9

F32 = jnp.float32
BF16 = jnp.bfloat16
NT = (((1,), (1,)), ((), ()))
TN = (((0,), (0,)), ((), ()))

PROJECTION_BITS = (2, 0)
OUT_BIT = 1

def dot(left, right):
    return jnp.dot(left, right, preferred_element_type=F32)


def dot_nt(left, right):
    return lax.dot_general(left, right, NT, preferred_element_type=F32)


def dot_tn(left, right):
    return lax.dot_general(left, right, TN, preferred_element_type=F32)


def call(
    body,
    name,
    inputs,
    outs,
    scratch=(),
    work=0,
    scalars=0,
    far=0,
    far_outs=0,
    after=(),
    vmem=VMEM_BYTES,
):
    near = len(inputs) - scalars - far
    count = len(inputs)
    specs = [pl.BlockSpec(memory_space=pltpu.SMEM)] * scalars
    specs += [pl.BlockSpec(memory_space=pltpu.VMEM)] * near
    specs += [pl.BlockSpec(memory_space=pltpu.HBM)] * (far + len(after))

    def run(*refs):
        body(*refs[:count], *refs[count + len(after) :])

    return pl.pallas_call(
        run,
        name=name,
        out_shape=outs,
        in_specs=specs,
        out_specs=[pl.BlockSpec(memory_space=pltpu.VMEM)] * (len(outs) - far_outs)
        + [pl.BlockSpec(memory_space=pltpu.HBM)] * far_outs,
        scratch_shapes=list(scratch),
        compiler_params=pltpu.CompilerParams(vmem_limit_bytes=vmem),
        cost_estimate=pl.CostEstimate(flops=work, bytes_accessed=0, transcendentals=0),
    )(*inputs, *after)


def fetch(pairs, sems, first=0):
    copies = [
        pltpu.make_async_copy(source, target, sems.at[first + place])
        for place, (source, target) in enumerate(pairs)
    ]
    for copy in copies:
        copy.start()
    return copies


def finish(copies):
    for copy in copies:
        copy.wait()


def spread(bits):
    found = [0]
    for bit in bits:
        found = [index | (value << bit) for index in found for value in (0, 1)]
    return found


def groups(bits, bit_count):
    others = [bit for bit in range(bit_count) if bit not in bits]
    return [[base | part for part in spread(bits)] for base in spread(others)]


def copy_chunks(source, target, chunks, size):
    for place, chunk in enumerate(chunks):
        target[place * size : (place + 1) * size, :] = source[chunk * size : (chunk + 1) * size, :]


def bit_here(bit):
    return (lax.axis_index("dp") >> bit) & 1


def prep_body(chunks, hidden, grad, x_blocks, g_send, x, g, turned, sides, sems):
    columns = g_send.shape[1]
    away = pl.ds(pl.multiple_of((1 - bit_here(OUT_BIT)) * columns, columns), columns)
    x_copy, g_copy = fetch([(hidden, x), (grad.at[:, away], g)], sems)
    x_copy.wait()
    turned[...] = x[...].astype(F32).T.astype(BF16)
    sends = []
    for row in range(2):
        own = [chunk | row << PROJECTION_BITS[0] for chunk in chunks]
        copy_chunks(turned, sides.at[row], own, turned.shape[0] // (2 * len(own)))
        pairs = [(sides.at[row], x_blocks.at[2 * col + row]) for col in range(2)]
        sends += fetch(pairs, sems, 2 + 2 * row)
    g_copy.wait()
    sends += fetch([(g, g_send)], sems, 6)
    finish(sends)


def seen_mask(pattern, seq_len, blocks, slots):
    block_len = seq_len // blocks
    rows = lax.broadcasted_iota(jnp.int32, (seq_len, seq_len), 0)
    columns = lax.broadcasted_iota(jnp.int32, (seq_len, seq_len), 1)
    row_block, column_block = rows // block_len, columns // block_len
    seen = jnp.zeros((seq_len, seq_len), F32)
    for block in range(blocks):
        for slot in range(slots):
            hit = (row_block == block) & (column_block == pattern[block, slot])
            seen = jnp.where(hit, 1.0, seen)
    return jnp.where((row_block == column_block) & (columns > rows), 0.0, seen)


def scale_of(x):
    return lax.rsqrt(jnp.mean(x * x, axis=-1, keepdims=True) + NORM_EPS)


def attention_body(
    out_chunks,
    pattern,
    x_own,
    x_mirror,
    w_query,
    w_key,
    w_value,
    g_own,
    g_mirror,
    w_out,
    attended,
    att_turned,
    blocks,
    x_all,
    weights,
    weight_out,
    g_all,
    query,
    key,
    values,
    grad_att,
    turned,
    sems,
):
    seq_len = x_own.shape[0]
    tokens = 2 * seq_len
    half = w_query.shape[1]
    own, other = pl.ds(0, seq_len), pl.ds(seq_len, seq_len)
    copies = fetch(
        [
            (x_own, x_all.at[own]),
            (x_mirror, x_all.at[other]),
            (w_query, weights.at[0]),
            (w_key, weights.at[1]),
            (w_value, weights.at[2]),
            (g_own, g_all.at[own]),
            (g_mirror, g_all.at[other]),
            (w_out, weight_out),
        ],
        sems,
    )
    finish(copies[:2])
    x = x_all[...]
    factor = scale_of(x.astype(F32))
    for place, target in enumerate((query, key, values)):
        copies[2 + place].wait()
        target[...] = (dot(x, weights[place]) * factor).astype(BF16)
    finish(copies[5:])
    grad_att[...] = dot_nt(g_all[...], weight_out[...]).astype(BF16)

    seen = seen_mask(pattern, seq_len, pattern.shape[0], pattern.shape[1])
    seen = jnp.concatenate([seen, seen], axis=0) > 0.0
    low = lax.broadcasted_iota(jnp.int32, (seq_len, PAIR), 1) < HDIM
    inv_sqrt = 1.0 / math.sqrt(HDIM)
    zero = jnp.zeros((), BF16)

    def stacked(block):
        return jnp.concatenate([jnp.where(low, block, zero), jnp.where(low, zero, block)], axis=0)

    def merged(both):
        return jnp.where(low, both[:seq_len], both[seq_len:])

    width = half // 2
    def put(member, col, first, here, value):
        rounded = value.astype(BF16)
        first += member * tokens
        for row in range(2):
            blocks[2 * col + row, first : first + seq_len, here] = rounded

    for pair in range(half // PAIR):
        columns = slice(pair * PAIR, (pair + 1) * PAIR)
        col, start = pair * PAIR // width, pair * PAIR % width
        here = slice(start, start + PAIR)
        for seq in range(2):
            rows = slice(seq * seq_len, (seq + 1) * seq_len)
            q2 = stacked(query[rows, columns])
            k = key[rows, columns]
            v = values[rows, columns]
            ga2 = stacked(grad_att[rows, columns])
            r = factor[rows]

            expo = jnp.where(seen, jnp.exp(dot_nt(q2, k) * inv_sqrt), 0.0)
            prob = expo / jnp.sum(expo, axis=-1, keepdims=True)
            prob_bf = prob.astype(BF16)
            attended[rows, columns] = merged(dot(prob_bf, v)).astype(BF16)
            grad_prob = dot_nt(ga2, v)
            inner = jnp.sum(prob * grad_prob, axis=-1, keepdims=True)
            score = (prob * (grad_prob - inner) * inv_sqrt).astype(BF16)
            put(0, col, seq * seq_len, here, dot_tn(prob_bf, ga2) * r)
            put(1, col, seq * seq_len, here, dot_tn(score, q2) * r)
            put(2, col, seq * seq_len, here, merged(dot(score, k)) * r)

    turned[...] = attended[...].astype(F32).T.astype(BF16)
    copy_chunks(turned, att_turned, out_chunks, half // len(out_chunks))


def returned_body(
    x_own,
    x_mirror,
    attended,
    w_out,
    w_query,
    w_key,
    w_value,
    blocks,
    contrib_own,
    contrib_mirror,
    returned_own,
    returned_mirror,
    x_all,
    att,
    weight_out,
    weights,
    grads,
    sems,
):
    seq_len = x_own.shape[0]
    tokens, half = att.shape
    width = half // 2
    pairs = [
        (attended, att),
        (w_out, weight_out),
        (x_own, x_all.at[pl.ds(0, seq_len)]),
        (x_mirror, x_all.at[pl.ds(seq_len, seq_len)]),
    ]
    for member in range(3):
        for col in range(2):
            source = blocks.at[2 * col, pl.ds(member * tokens, tokens)]
            pairs.append((source, grads.at[member, :, pl.ds(col * width, width)]))
    pairs += [(w_value, weights.at[0]), (w_key, weights.at[1]), (w_query, weights.at[2])]
    copies = fetch(pairs, sems)
    finish(copies[:2])
    contrib = dot(att[...], weight_out[...]).astype(BF16)
    contrib_own[...] = contrib[:seq_len]
    contrib_mirror[...] = contrib[seq_len:]
    finish(copies[2:-3])
    grad = None
    for member in range(3):
        copies[member - 3].wait()
        term = dot_nt(grads[member], weights[member])
        grad = term if grad is None else grad + term
    x = x_all[...].astype(F32)
    factor = scale_of(x)
    mean_term = jnp.mean(x * grad, axis=-1, keepdims=True)
    returned = (grad - x * (factor * factor * mean_term)).astype(BF16)
    returned_own[...] = returned[:seq_len]
    returned_mirror[...] = returned[seq_len:]


def projection_grad_body(bits, x_pieces, x_mirrors, g_pieces, *rest):
    pair_send, pair_keep, query_send, query_keep, x_all, right, pair_sums, query_sums, sems = rest
    seq_len = x_pieces.shape[2]
    tokens = 2 * seq_len
    width = g_pieces.shape[2]
    pairs = []
    for place in range(4):
        for at, source in enumerate((x_pieces, x_mirrors)):
            columns = pl.ds(place * tokens + at * seq_len, seq_len)
            pairs.append((source.at[place], x_all.at[:, columns]))
        for member in range(3):
            target = right.at[pl.ds(place * tokens, tokens), pl.ds(member * width, width)]
            pairs.append((g_pieces.at[place, pl.ds(member * tokens, tokens)], target))
    copies = fetch(pairs, sems)
    rows = x_all.shape[0] // 2
    pair_bit, query_bit = bit_here(bits[0]), bit_here(bits[1])
    count = 1 << (len(bits) - 2)
    size = rows // 2 // count
    middle = 2 * tokens
    for half_at, depth in enumerate((slice(0, middle), slice(middle, 2 * middle))):
        finish(copies[10 * half_at : 10 * (half_at + 1)])
        for at, (target, side) in enumerate(((pair_send, 1 - pair_bit), (pair_keep, pair_bit))):
            part = pl.ds(pl.multiple_of(side * rows, rows), rows)
            grad = dot(x_all[part, depth], right[depth, : 2 * width])
            if half_at == 0:
                pair_sums[at] = grad
            else:
                target[...] = (pair_sums[at] + grad).astype(BF16)
        for at, (target, side) in enumerate(((query_send, 1 - query_bit), (query_keep, query_bit))):
            for turn in range(2):
                for place in range(count):
                    start = turn * rows + side * (rows // 2) + place * size
                    part = pl.ds(pl.multiple_of(start, size), size)
                    grad = dot(x_all[part, depth], right[depth, 2 * width :])
                    here = slice((2 * place + turn) * size, (2 * place + turn + 1) * size)
                    if half_at == 0:
                        query_sums[at, here, :] = grad
                    else:
                        target[here, :] = (query_sums[at, here, :] + grad).astype(BF16)


def out_grad_body(bits, grad, g_mirror, g_piece, g_piece_mirror, att_own, att_piece, *rest):
    targets, (left, right, sems) = rest[:4], rest[4:]
    seq_len = grad.shape[0]
    tokens = 2 * seq_len
    columns = right.shape[1]
    here = pl.ds(pl.multiple_of(bit_here(OUT_BIT) * columns, columns), columns)
    pairs = [
        (att_own, left.at[:, pl.ds(0, tokens)]),
        (att_piece, left.at[:, pl.ds(tokens, tokens)]),
    ]
    for place, source in enumerate(
        (grad.at[:, here], g_mirror.at[:, here], g_piece, g_piece_mirror)
    ):
        pairs.append((source, right.at[pl.ds(place * seq_len, seq_len)]))
    finish(fetch(pairs, sems))
    own = 2 * bit_here(bits[0]) + bit_here(bits[1])
    rows = left.shape[0] // 4
    for place, target in enumerate(targets):
        part = pl.ds(pl.multiple_of((own ^ place) * rows, rows), rows)
        target[...] = dot(left[part, :], right[...]).astype(BF16)


def halve_body(bit, count, *refs):
    sources, (send, keep, sides, sems) = refs[:count], refs[count:]
    here = bit_here(bit)
    rows = send.shape[0]
    pairs = []
    for turn, side in ((0, 1 - here), (1, here)):
        part = pl.ds(pl.multiple_of(side * rows, rows), rows)
        pairs += [(ref.at[part], sides.at[turn, at]) for at, ref in enumerate(sources)]
    copies = fetch(pairs, sems)
    for turn, target in ((0, send), (1, keep)):
        finish(copies[turn * count : (turn + 1) * count])
        total = sides[turn, 0].astype(F32)
        for at in range(1, count):
            total += sides[turn, at].astype(F32)
        target[...] = total.astype(BF16)


def meet_body(
    col_bit, query_keep, query_arrived, out_keep, out_arrived, own, send_out, send_col, send_both, *rest
):
    next_out, query, out, sems = rest
    here = bit_here(OUT_BIT)
    col = bit_here(col_bit)
    rows, out_rows, width = own.shape[0], next_out.shape[0], own.shape[1]
    copies = fetch(
        [
            (query_keep, query.at[0]),
            (query_arrived, query.at[1]),
            (out_keep, out.at[0]),
            (out_arrived, out.at[1]),
        ],
        sems,
    )

    def total(both, block, extent):
        part = pl.ds(pl.multiple_of(block * extent, extent), extent)
        return (both[0, part, :].astype(F32) + both[1, part, :].astype(F32)).astype(BF16)

    finish(copies[:2])
    own[...] = total(query, 2 * here + col, rows)
    send_out[:rows, :] = total(query, 2 * (1 - here) + col, rows)
    send_col[...] = total(query, 2 * here + 1 - col, rows)
    send_both[...] = total(query, 2 * (1 - here) + 1 - col, rows)
    finish(copies[2:])
    away = total(out, 1 - here, out_rows)
    for place in range(next_out.shape[1] // width):
        first = rows + place * out_rows
        send_out[first : first + out_rows, :] = away[:, place * width : (place + 1) * width]
    next_out[...] = total(out, here, out_rows)


def final_body(pieces, own, from_out, from_col, from_both, out_own, *targets):
    columns = targets[0].shape[1] // 2
    for col in range(2):
        total = pieces[col].astype(F32)
        for place in range(1, pieces.shape[0] // 2):
            total += pieces[2 * place + col].astype(F32)
        for member in range(2):
            targets[member][:, col * columns : (col + 1) * columns] = total[
                :, member * columns : (member + 1) * columns
            ]
    here = bit_here(PROJECTION_BITS[1])
    rows = own.shape[0]
    for one, two, col in ((own, from_out, here), (from_col, from_both, 1 - here)):
        place = pl.ds(pl.multiple_of(col * columns, columns), columns)
        targets[2][:, place] = one[...].astype(F32) + two[:rows, :].astype(F32)
    here = bit_here(OUT_BIT)
    out_rows, out_columns = out_own.shape
    place = pl.ds(pl.multiple_of(here * out_columns, out_columns), out_columns)
    targets[3][:, place] = out_own[...].astype(F32)
    for at in range(out_columns // columns):
        start = (1 - here) * out_columns + at * columns
        first = rows + at * out_rows
        block = from_out[first : first + out_rows, :].astype(F32)
        targets[3][:, pl.ds(pl.multiple_of(start, columns), columns)] = block


def on_device(hidden_in, grad_out, w_query, w_key, w_value, w_out, pattern):
    replicas = lax.axis_size("dp")
    pipe = lax.axis_size("pipe")
    bit_count = replicas.bit_length() - 1
    row_bit, col_bit = PROJECTION_BITS
    halved_bits = [bit for bit in range(bit_count) if bit not in PROJECTION_BITS]
    out_bits = [col_bit, row_bit] + [bit for bit in halved_bits if bit != OUT_BIT]
    chunks = spread(halved_bits + [col_bit])
    out_chunks = spread(out_bits + [OUT_BIT])
    seq_len, features = hidden_in.shape
    half = w_query.shape[2]
    w_query, w_key, w_value, w_out = w_query[0], w_key[0], w_value[0], w_out[0]
    width, part, tokens = half // 2, features // 2, 2 * seq_len

    def swap(x, *bits):
        apart = sum(1 << bit for bit in bits)
        return lax.ppermute(x, "dp", [(i, i ^ apart) for i in range(replicas)])

    def mirror(x):
        return lax.ppermute(x, "pipe", [(i, pipe - 1 - i) for i in range(pipe)])

    def exchange(x, bits):
        members = groups(bits, bit_count)
        return lax.all_to_all(x, "dp", 0, 0, axis_index_groups=members, tiled=True)

    def follows(x, before):
        return lax.optimization_barrier((x, before))[0]

    def bf16(*shape):
        return jax.ShapeDtypeStruct(shape, BF16)

    x_mirror = mirror(hidden_in)
    g_mirror = mirror(grad_out)
    x_blocks, g_send = call(
        functools.partial(prep_body, chunks),
        "prep",
        (hidden_in, grad_out),
        [bf16(4, part, seq_len), bf16(seq_len, part)],
        [
            pltpu.VMEM((seq_len, features), BF16),
            pltpu.VMEM((seq_len, part), BF16),
            pltpu.VMEM((features, seq_len), BF16),
            pltpu.VMEM((2, part, seq_len), BF16),
            pltpu.SemaphoreType.DMA((7,)),
        ],
        far=2,
        far_outs=2,
    )
    x_pieces = exchange(x_blocks, [col_bit, row_bit])
    g_piece = swap(g_send, OUT_BIT)

    attended, att_turned, g_blocks = call(
        functools.partial(attention_body, out_chunks),
        "attention",
        (pattern, hidden_in, x_mirror, w_query, w_key, w_value, grad_out, g_mirror, w_out),
        [bf16(tokens, half), bf16(half, tokens)]
        + [bf16(4, 3 * tokens, width)],
        [
            pltpu.VMEM((tokens, features), BF16),
            pltpu.VMEM((3, features, half), BF16),
            pltpu.VMEM((half, features), BF16),
            pltpu.VMEM((tokens, features), BF16),
        ]
        + [pltpu.VMEM((tokens, half), BF16)] * 4
        + [
            pltpu.VMEM((half, tokens), BF16),
            pltpu.SemaphoreType.DMA((8,)),
        ],
        work=LONG_WORK,
        scalars=1,
        far=8,
        after=(x_blocks,),
    )
    g_pieces = exchange(follows(g_blocks, g_piece), [col_bit, row_bit])
    att_piece = swap(att_turned, OUT_BIT)
    x_mirrors = mirror(follows(x_pieces, attended))
    g_piece_mirror = mirror(follows(g_piece, attended))

    contrib, contrib_mirror, returned, returned_mirror = call(
        returned_body,
        "returned",
        (hidden_in, x_mirror, attended, w_out, w_query, w_key, w_value, g_blocks),
        [bf16(seq_len, features)] * 4,
        [
            pltpu.VMEM((tokens, features), BF16),
            pltpu.VMEM((tokens, half), BF16),
            pltpu.VMEM((half, features), BF16),
            pltpu.VMEM((3, features, half), BF16),
            pltpu.VMEM((3, tokens, half), BF16),
            pltpu.SemaphoreType.DMA((13,)),
        ],
        far=8,
    )

    out_keep, *out_sends = call(
        functools.partial(out_grad_body, out_bits[:2]),
        "out_grad",
        (grad_out, g_mirror, g_piece, g_piece_mirror, att_turned, att_piece),
        [bf16(half // 4, part)] * 4,
        [
            pltpu.VMEM((half, 2 * tokens), BF16),
            pltpu.VMEM((2 * tokens, part), BF16),
            pltpu.SemaphoreType.DMA((6,)),
        ],
        far=6,
        after=(contrib, x_mirrors),
    )
    out_arrived = [
        swap(out_sends[0], out_bits[1]),
        swap(out_sends[1], out_bits[0]),
        swap(out_sends[2], *out_bits[:2]),
    ]
    pair_send, pair_keep, query_send, query_keep = call(
        functools.partial(projection_grad_body, halved_bits),
        "projection_grad",
        (x_pieces, x_mirrors, g_pieces),
        [bf16(part // 2, 2 * width)] * 2 + [bf16(part // 2, width)] * 2,
        [
            pltpu.VMEM((part, 4 * tokens), BF16),
            pltpu.VMEM((4 * tokens, 3 * width), BF16),
            pltpu.VMEM((2, part // 2, 2 * width), F32),
            pltpu.VMEM((2, part // 2, width), F32),
            pltpu.SemaphoreType.DMA((20,)),
        ],
        far=3,
        after=(out_keep,),
        vmem=LATE_VMEM_BYTES,
    )
    pair_arrived = swap(pair_send, halved_bits[0])
    query_arrived = swap(query_send, halved_bits[1])

    def halve(arrays, next_bit, after, work=0):
        count, shape = len(arrays), (arrays[0].shape[0] // 2, arrays[0].shape[1])
        return call(
            functools.partial(halve_body, next_bit, count),
            "halve",
            arrays,
            [bf16(*shape)] * 2,
            [pltpu.VMEM((2, count, *shape), BF16), pltpu.SemaphoreType.DMA((2 * count,))],
            work=work,
            far=count,
            vmem=LATE_VMEM_BYTES,
            after=(after,),
        )

    def stepped(arrays, bits, after, work=0):
        send, keep = halve(arrays, bits[0], after, work)
        return [keep, swap(send, bits[0])], bits[1:], send

    out, out_left, last = stepped(
        [out_keep] + out_arrived, out_bits[2:] + [OUT_BIT], pair_send, LONG_WORK
    )
    contrib_other = mirror(follows(contrib_mirror, last))
    returned_other = mirror(follows(returned_mirror, last))
    hidden_out = (
        hidden_in.astype(F32) + contrib.astype(F32) + contrib_other.astype(F32)
    ).astype(BF16)
    grad_in = (
        grad_out.astype(F32) + returned.astype(F32) + returned_other.astype(F32)
    ).astype(BF16)

    pair_total = pair_keep.astype(F32) + follows(pair_arrived, (last, query_arrived)).astype(F32)
    pair_total = pair_total.astype(BF16)
    pieces = exchange(pair_total, halved_bits[1:] + [col_bit])
    last = pair_total
    while out_left[1:]:
        out, out_left, last = stepped(out, out_left, last)
    query = [query_keep, query_arrived]
    for bit in halved_bits[2:]:
        query, _, last = stepped(query, [bit], last)
    rows, out_rows = features // replicas, half // replicas
    own, send_out, send_col, send_both, out_own = call(
        functools.partial(meet_body, col_bit),
        "meet",
        (*query, *out),
        [bf16(rows, width), bf16(rows + out_rows * (part // width), width)]
        + [bf16(rows, width)] * 2
        + [bf16(out_rows, part)],
        [
            pltpu.VMEM((2, 4 * rows, width), BF16),
            pltpu.VMEM((2, 2 * out_rows, part), BF16),
            pltpu.SemaphoreType.DMA((4,)),
        ],
        far=4,
        after=(last,),
        vmem=LATE_VMEM_BYTES,
    )
    blocks = [
        own,
        swap(send_out, OUT_BIT),
        swap(send_col, col_bit),
        swap(send_both, OUT_BIT, col_bit),
        out_own,
    ]
    grads = call(
        final_body,
        "final",
        (pieces.reshape(1 << len(halved_bits), -1, 2 * width), *blocks),
        [jax.ShapeDtypeStruct((rows, half), F32)] * 3
        + [jax.ShapeDtypeStruct((out_rows, features), F32)],
        vmem=LATE_VMEM_BYTES,
    )
    grad_value, grad_key, grad_query, grad_wout = (grad[None] for grad in grads)
    return (hidden_out, grad_in, grad_query, grad_key, grad_value, grad_wout)


def solution(mesh):
    in_specs = (
        P(("dp", "pipe"), None),
        P(("dp", "pipe"), None),
        P("pipe", None, None),
        P("pipe", None, None),
        P("pipe", None, None),
        P("pipe", None, None),
        P(),
    )
    out_specs = (
        P(("dp", "pipe"), None),
        P(("dp", "pipe"), None),
        P("pipe", "dp", None),
        P("pipe", "dp", None),
        P("pipe", "dp", None),
        P("pipe", "dp", None),
    )
    return jax.shard_map(
        on_device, mesh=mesh, in_specs=in_specs, out_specs=out_specs, check_vma=False
    )
```

```python
import functools
import math

import jax
import jax.numpy as jnp
from jax import lax
from jax.experimental import pallas as pl
from jax.experimental.pallas import tpu as pltpu
from jax.sharding import PartitionSpec as P

HDIM = 64
NORM_EPS = 1e-05
PAIR = 2 * HDIM
VMEM_BYTES = 64 * 1024 * 1024

LATE_VMEM_BYTES = 16 * 1024 * 1024

LONG_WORK = 11 * 10**9

F32 = jnp.float32
BF16 = jnp.bfloat16
NT = (((1,), (1,)), ((), ()))
TN = (((0,), (0,)), ((), ()))

PROJECTION_BITS = (2, 0)
OUT_BIT = 1

def dot(left, right):
    return jnp.dot(left, right, preferred_element_type=F32)


def dot_nt(left, right):
    return lax.dot_general(left, right, NT, preferred_element_type=F32)


def dot_tn(left, right):
    return lax.dot_general(left, right, TN, preferred_element_type=F32)


def call(
    body,
    name,
    inputs,
    outs,
    scratch=(),
    work=0,
    scalars=0,
    far=0,
    far_outs=0,
    after=(),
    vmem=VMEM_BYTES,
):
    near = len(inputs) - scalars - far
    count = len(inputs)
    specs = [pl.BlockSpec(memory_space=pltpu.SMEM)] * scalars
    specs += [pl.BlockSpec(memory_space=pltpu.VMEM)] * near
    specs += [pl.BlockSpec(memory_space=pltpu.HBM)] * (far + len(after))

    def run(*refs):
        body(*refs[:count], *refs[count + len(after) :])

    return pl.pallas_call(
        run,
        name=name,
        out_shape=outs,
        in_specs=specs,
        out_specs=[pl.BlockSpec(memory_space=pltpu.VMEM)] * (len(outs) - far_outs)
        + [pl.BlockSpec(memory_space=pltpu.HBM)] * far_outs,
        scratch_shapes=list(scratch),
        compiler_params=pltpu.CompilerParams(vmem_limit_bytes=vmem),
        cost_estimate=pl.CostEstimate(flops=work, bytes_accessed=0, transcendentals=0),
    )(*inputs, *after)


def fetch(pairs, sems, first=0):
    copies = [
        pltpu.make_async_copy(source, target, sems.at[first + place])
        for place, (source, target) in enumerate(pairs)
    ]
    for copy in copies:
        copy.start()
    return copies


def finish(copies):
    for copy in copies:
        copy.wait()


def spread(bits):
    found = [0]
    for bit in bits:
        found = [index | (value << bit) for index in found for value in (0, 1)]
    return found


def groups(bits, bit_count):
    others = [bit for bit in range(bit_count) if bit not in bits]
    return [[base | part for part in spread(bits)] for base in spread(others)]


def copy_chunks(source, target, chunks, size):
    for place, chunk in enumerate(chunks):
        target[place * size : (place + 1) * size, :] = source[chunk * size : (chunk + 1) * size, :]


def bit_here(bit):
    return (lax.axis_index("dp") >> bit) & 1


def prep_body(chunks, hidden, grad, x_blocks, g_send, x, g, turned, sides, sems):
    columns = g_send.shape[1]
    away = pl.ds(pl.multiple_of((1 - bit_here(OUT_BIT)) * columns, columns), columns)
    x_copy, g_copy = fetch([(hidden, x), (grad.at[:, away], g)], sems)
    x_copy.wait()
    turned[...] = x[...].T
    sends = []
    for row in range(2):
        own = [chunk | row << PROJECTION_BITS[0] for chunk in chunks]
        copy_chunks(turned, sides.at[row], own, turned.shape[0] // (2 * len(own)))
        pairs = [(sides.at[row], x_blocks.at[2 * col + row]) for col in range(2)]
        sends += fetch(pairs, sems, 2 + 2 * row)
    g_copy.wait()
    sends += fetch([(g, g_send)], sems, 6)
    finish(sends)


def seen_mask(pattern, seq_len, blocks, slots):
    block_len = seq_len // blocks
    rows = lax.broadcasted_iota(jnp.int32, (seq_len, seq_len), 0)
    columns = lax.broadcasted_iota(jnp.int32, (seq_len, seq_len), 1)
    row_block, column_block = rows // block_len, columns // block_len
    seen = jnp.zeros((seq_len, seq_len), F32)
    for block in range(blocks):
        for slot in range(slots):
            hit = (row_block == block) & (column_block == pattern[block, slot])
            seen = jnp.where(hit, 1.0, seen)
    return jnp.where((row_block == column_block) & (columns > rows), 0.0, seen)


def scale_of(x):
    return lax.rsqrt(jnp.mean(x * x, axis=-1, keepdims=True) + NORM_EPS)


def attention_body(
    out_chunks,
    pattern,
    x_own,
    x_mirror,
    w_query,
    w_key,
    w_value,
    g_own,
    g_mirror,
    w_out,
    attended,
    att_turned,
    blocks,
    x_all,
    weights,
    weight_out,
    g_all,
    query,
    key,
    values,
    grad_att,
    turned,
    sems,
):
    seq_len = x_own.shape[0]
    tokens = 2 * seq_len
    half = w_query.shape[1]
    own, other = pl.ds(0, seq_len), pl.ds(seq_len, seq_len)
    copies = fetch(
        [
            (x_own, x_all.at[own]),
            (x_mirror, x_all.at[other]),
            (w_query, weights.at[0]),
            (w_key, weights.at[1]),
            (w_value, weights.at[2]),
            (g_own, g_all.at[own]),
            (g_mirror, g_all.at[other]),
            (w_out, weight_out),
        ],
        sems,
    )
    finish(copies[:2])
    x = x_all[...]
    factor = scale_of(x.astype(F32))
    for place, target in enumerate((query, key, values)):
        copies[2 + place].wait()
        target[...] = (dot(x, weights[place]) * factor).astype(BF16)
    finish(copies[5:])
    grad_att[...] = dot_nt(g_all[...], weight_out[...]).astype(BF16)

    seen = seen_mask(pattern, seq_len, pattern.shape[0], pattern.shape[1])
    seen = jnp.concatenate([seen, seen], axis=0) > 0.0
    low = lax.broadcasted_iota(jnp.int32, (seq_len, PAIR), 1) < HDIM
    inv_sqrt = 1.0 / math.sqrt(HDIM)
    zero = jnp.zeros((), BF16)

    def stacked(block):
        return jnp.concatenate([jnp.where(low, block, zero), jnp.where(low, zero, block)], axis=0)

    def merged(both):
        return jnp.where(low, both[:seq_len], both[seq_len:])

    width = half // 2
    def put(member, col, first, here, value):
        rounded = value.astype(BF16)
        first += member * tokens
        for row in range(2):
            blocks[2 * col + row, first : first + seq_len, here] = rounded

    for pair in range(half // PAIR):
        columns = slice(pair * PAIR, (pair + 1) * PAIR)
        col, start = pair * PAIR // width, pair * PAIR % width
        here = slice(start, start + PAIR)
        for seq in range(2):
            rows = slice(seq * seq_len, (seq + 1) * seq_len)
            q2 = stacked(query[rows, columns])
            k = key[rows, columns]
            v = values[rows, columns]
            ga2 = stacked(grad_att[rows, columns])
            r = factor[rows]

            expo = jnp.where(seen, jnp.exp(dot_nt(q2, k) * inv_sqrt), 0.0)
            prob = expo / jnp.sum(expo, axis=-1, keepdims=True)
            prob_bf = prob.astype(BF16)
            attended[rows, columns] = merged(dot(prob_bf, v)).astype(BF16)
            grad_prob = dot_nt(ga2, v)
            inner = jnp.sum(prob * grad_prob, axis=-1, keepdims=True)
            score = (prob * (grad_prob - inner) * inv_sqrt).astype(BF16)
            put(0, col, seq * seq_len, here, dot_tn(prob_bf, ga2) * r)
            put(1, col, seq * seq_len, here, dot_tn(score, q2) * r)
            put(2, col, seq * seq_len, here, merged(dot(score, k)) * r)

    turned[...] = attended[...].T
    copy_chunks(turned, att_turned, out_chunks, half // len(out_chunks))


def returned_body(
    x_own,
    x_mirror,
    attended,
    w_out,
    w_query,
    w_key,
    w_value,
    blocks,
    contrib_own,
    contrib_mirror,
    returned_own,
    returned_mirror,
    x_all,
    att,
    weight_out,
    weights,
    grads,
    sems,
):
    seq_len = x_own.shape[0]
    tokens, half = att.shape
    width = half // 2
    pairs = [
        (attended, att),
        (w_out, weight_out),
        (x_own, x_all.at[pl.ds(0, seq_len)]),
        (x_mirror, x_all.at[pl.ds(seq_len, seq_len)]),
    ]
    for member in range(3):
        for col in range(2):
            source = blocks.at[2 * col, pl.ds(member * tokens, tokens)]
            pairs.append((source, grads.at[member, :, pl.ds(col * width, width)]))
    pairs += [(w_value, weights.at[0]), (w_key, weights.at[1]), (w_query, weights.at[2])]
    copies = fetch(pairs, sems)
    finish(copies[:2])
    contrib = dot(att[...], weight_out[...]).astype(BF16)
    contrib_own[...] = contrib[:seq_len]
    contrib_mirror[...] = contrib[seq_len:]
    finish(copies[2:-3])
    grad = None
    for member in range(3):
        copies[member - 3].wait()
        term = dot_nt(grads[member], weights[member])
        grad = term if grad is None else grad + term
    x = x_all[...].astype(F32)
    factor = scale_of(x)
    mean_term = jnp.mean(x * grad, axis=-1, keepdims=True)
    returned = (grad - x * (factor * factor * mean_term)).astype(BF16)
    returned_own[...] = returned[:seq_len]
    returned_mirror[...] = returned[seq_len:]


def projection_grad_body(bits, x_pieces, x_mirrors, g_pieces, *rest):
    pair_send, pair_keep, query_send, query_keep, x_all, right, pair_sums, query_sums, sems = rest
    seq_len = x_pieces.shape[2]
    tokens = 2 * seq_len
    width = g_pieces.shape[2]
    pairs = []
    for place in range(4):
        for at, source in enumerate((x_pieces, x_mirrors)):
            columns = pl.ds(place * tokens + at * seq_len, seq_len)
            pairs.append((source.at[place], x_all.at[:, columns]))
        for member in range(3):
            target = right.at[pl.ds(place * tokens, tokens), pl.ds(member * width, width)]
            pairs.append((g_pieces.at[place, pl.ds(member * tokens, tokens)], target))
    copies = fetch(pairs, sems)
    rows = x_all.shape[0] // 2
    pair_bit, query_bit = bit_here(bits[0]), bit_here(bits[1])
    count = 1 << (len(bits) - 2)
    size = rows // 2 // count
    middle = 2 * tokens
    for half_at, depth in enumerate((slice(0, middle), slice(middle, 2 * middle))):
        finish(copies[10 * half_at : 10 * (half_at + 1)])
        for at, (target, side) in enumerate(((pair_send, 1 - pair_bit), (pair_keep, pair_bit))):
            part = pl.ds(pl.multiple_of(side * rows, rows), rows)
            grad = dot(x_all[part, depth], right[depth, : 2 * width])
            if half_at == 0:
                pair_sums[at] = grad
            else:
                target[...] = (pair_sums[at] + grad).astype(BF16)
        for at, (target, side) in enumerate(((query_send, 1 - query_bit), (query_keep, query_bit))):
            for turn in range(2):
                for place in range(count):
                    start = turn * rows + side * (rows // 2) + place * size
                    part = pl.ds(pl.multiple_of(start, size), size)
                    grad = dot(x_all[part, depth], right[depth, 2 * width :])
                    here = slice((2 * place + turn) * size, (2 * place + turn + 1) * size)
                    if half_at == 0:
                        query_sums[at, here, :] = grad
                    else:
                        target[here, :] = (query_sums[at, here, :] + grad).astype(BF16)


def out_grad_body(bits, grad, g_mirror, g_piece, g_piece_mirror, att_own, att_piece, *rest):
    targets, (left, right, sems) = rest[:4], rest[4:]
    seq_len = grad.shape[0]
    tokens = 2 * seq_len
    columns = right.shape[1]
    here = pl.ds(pl.multiple_of(bit_here(OUT_BIT) * columns, columns), columns)
    pairs = [
        (att_own, left.at[:, pl.ds(0, tokens)]),
        (att_piece, left.at[:, pl.ds(tokens, tokens)]),
    ]
    for place, source in enumerate(
        (grad.at[:, here], g_mirror.at[:, here], g_piece, g_piece_mirror)
    ):
        pairs.append((source, right.at[pl.ds(place * seq_len, seq_len)]))
    finish(fetch(pairs, sems))
    own = 2 * bit_here(bits[0]) + bit_here(bits[1])
    rows = left.shape[0] // 4
    for place, target in enumerate(targets):
        part = pl.ds(pl.multiple_of((own ^ place) * rows, rows), rows)
        target[...] = dot(left[part, :], right[...]).astype(BF16)


def halve_body(bit, count, *refs):
    sources, (send, keep, sides, sems) = refs[:count], refs[count:]
    here = bit_here(bit)
    rows = send.shape[0]
    pairs = []
    for turn, side in ((0, 1 - here), (1, here)):
        part = pl.ds(pl.multiple_of(side * rows, rows), rows)
        pairs += [(ref.at[part], sides.at[turn, at]) for at, ref in enumerate(sources)]
    copies = fetch(pairs, sems)
    for turn, target in ((0, send), (1, keep)):
        finish(copies[turn * count : (turn + 1) * count])
        total = sides[turn, 0].astype(F32)
        for at in range(1, count):
            total += sides[turn, at].astype(F32)
        target[...] = total.astype(BF16)


def meet_body(
    col_bit, query_keep, query_arrived, out_keep, out_arrived, own, send_out, send_col, send_both, *rest
):
    next_out, query, out, sems = rest
    here = bit_here(OUT_BIT)
    col = bit_here(col_bit)
    rows, out_rows, width = own.shape[0], next_out.shape[0], own.shape[1]
    copies = fetch(
        [
            (query_keep, query.at[0]),
            (query_arrived, query.at[1]),
            (out_keep, out.at[0]),
            (out_arrived, out.at[1]),
        ],
        sems,
    )

    def total(both, block, extent):
        part = pl.ds(pl.multiple_of(block * extent, extent), extent)
        return (both[0, part, :].astype(F32) + both[1, part, :].astype(F32)).astype(BF16)

    finish(copies[:2])
    own[...] = total(query, 2 * here + col, rows)
    send_out[:rows, :] = total(query, 2 * (1 - here) + col, rows)
    send_col[...] = total(query, 2 * here + 1 - col, rows)
    send_both[...] = total(query, 2 * (1 - here) + 1 - col, rows)
    finish(copies[2:])
    away = total(out, 1 - here, out_rows)
    for place in range(next_out.shape[1] // width):
        first = rows + place * out_rows
        send_out[first : first + out_rows, :] = away[:, place * width : (place + 1) * width]
    next_out[...] = total(out, here, out_rows)


def final_body(pieces, own, from_out, from_col, from_both, out_own, *targets):
    columns = targets[0].shape[1] // 2
    for col in range(2):
        total = pieces[col].astype(F32)
        for place in range(1, pieces.shape[0] // 2):
            total += pieces[2 * place + col].astype(F32)
        for member in range(2):
            targets[member][:, col * columns : (col + 1) * columns] = total[
                :, member * columns : (member + 1) * columns
            ]
    here = bit_here(PROJECTION_BITS[1])
    rows = own.shape[0]
    for one, two, col in ((own, from_out, here), (from_col, from_both, 1 - here)):
        place = pl.ds(pl.multiple_of(col * columns, columns), columns)
        targets[2][:, place] = one[...].astype(F32) + two[:rows, :].astype(F32)
    here = bit_here(OUT_BIT)
    out_rows, out_columns = out_own.shape
    place = pl.ds(pl.multiple_of(here * out_columns, out_columns), out_columns)
    targets[3][:, place] = out_own[...].astype(F32)
    for at in range(out_columns // columns):
        start = (1 - here) * out_columns + at * columns
        first = rows + at * out_rows
        block = from_out[first : first + out_rows, :].astype(F32)
        targets[3][:, pl.ds(pl.multiple_of(start, columns), columns)] = block


def on_device(hidden_in, grad_out, w_query, w_key, w_value, w_out, pattern):
    replicas = lax.axis_size("dp")
    pipe = lax.axis_size("pipe")
    bit_count = replicas.bit_length() - 1
    row_bit, col_bit = PROJECTION_BITS
    halved_bits = [bit for bit in range(bit_count) if bit not in PROJECTION_BITS]
    out_bits = [col_bit, row_bit] + [bit for bit in halved_bits if bit != OUT_BIT]
    chunks = spread(halved_bits + [col_bit])
    out_chunks = spread(out_bits + [OUT_BIT])
    seq_len, features = hidden_in.shape
    half = w_query.shape[2]
    w_query, w_key, w_value, w_out = w_query[0], w_key[0], w_value[0], w_out[0]
    width, part, tokens = half // 2, features // 2, 2 * seq_len

    def swap(x, *bits):
        apart = sum(1 << bit for bit in bits)
        return lax.ppermute(x, "dp", [(i, i ^ apart) for i in range(replicas)])

    def mirror(x):
        return lax.ppermute(x, "pipe", [(i, pipe - 1 - i) for i in range(pipe)])

    def exchange(x, bits):
        members = groups(bits, bit_count)
        return lax.all_to_all(x, "dp", 0, 0, axis_index_groups=members, tiled=True)

    def follows(x, before):
        return lax.optimization_barrier((x, before))[0]

    def bf16(*shape):
        return jax.ShapeDtypeStruct(shape, BF16)

    x_mirror = mirror(hidden_in)
    g_mirror = mirror(grad_out)
    x_blocks, g_send = call(
        functools.partial(prep_body, chunks),
        "prep",
        (hidden_in, grad_out),
        [bf16(4, part, seq_len), bf16(seq_len, part)],
        [
            pltpu.VMEM((seq_len, features), BF16),
            pltpu.VMEM((seq_len, part), BF16),
            pltpu.VMEM((features, seq_len), BF16),
            pltpu.VMEM((2, part, seq_len), BF16),
            pltpu.SemaphoreType.DMA((7,)),
        ],
        far=2,
        far_outs=2,
    )
    x_pieces = exchange(x_blocks, [col_bit, row_bit])
    g_piece = swap(g_send, OUT_BIT)

    attended, att_turned, g_blocks = call(
        functools.partial(attention_body, out_chunks),
        "attention",
        (pattern, hidden_in, x_mirror, w_query, w_key, w_value, grad_out, g_mirror, w_out),
        [bf16(tokens, half), bf16(half, tokens)]
        + [bf16(4, 3 * tokens, width)],
        [
            pltpu.VMEM((tokens, features), BF16),
            pltpu.VMEM((3, features, half), BF16),
            pltpu.VMEM((half, features), BF16),
            pltpu.VMEM((tokens, features), BF16),
        ]
        + [pltpu.VMEM((tokens, half), BF16)] * 4
        + [
            pltpu.VMEM((half, tokens), BF16),
            pltpu.SemaphoreType.DMA((8,)),
        ],
        work=LONG_WORK,
        scalars=1,
        far=8,
        after=(x_blocks,),
    )
    g_pieces = exchange(follows(g_blocks, g_piece), [col_bit, row_bit])
    att_piece = swap(att_turned, OUT_BIT)
    x_mirrors = mirror(follows(x_pieces, attended))
    g_piece_mirror = mirror(follows(g_piece, attended))

    contrib, contrib_mirror, returned, returned_mirror = call(
        returned_body,
        "returned",
        (hidden_in, x_mirror, attended, w_out, w_query, w_key, w_value, g_blocks),
        [bf16(seq_len, features)] * 4,
        [
            pltpu.VMEM((tokens, features), BF16),
            pltpu.VMEM((tokens, half), BF16),
            pltpu.VMEM((half, features), BF16),
            pltpu.VMEM((3, features, half), BF16),
            pltpu.VMEM((3, tokens, half), BF16),
            pltpu.SemaphoreType.DMA((13,)),
        ],
        far=8,
    )

    out_keep, *out_sends = call(
        functools.partial(out_grad_body, out_bits[:2]),
        "out_grad",
        (grad_out, g_mirror, g_piece, g_piece_mirror, att_turned, att_piece),
        [bf16(half // 4, part)] * 4,
        [
            pltpu.VMEM((half, 2 * tokens), BF16),
            pltpu.VMEM((2 * tokens, part), BF16),
            pltpu.SemaphoreType.DMA((6,)),
        ],
        far=6,
        after=(contrib, x_mirrors),
    )
    out_arrived = [
        swap(out_sends[0], out_bits[1]),
        swap(out_sends[1], out_bits[0]),
        swap(out_sends[2], *out_bits[:2]),
    ]
    pair_send, pair_keep, query_send, query_keep = call(
        functools.partial(projection_grad_body, halved_bits),
        "projection_grad",
        (x_pieces, x_mirrors, g_pieces),
        [bf16(part // 2, 2 * width)] * 2 + [bf16(part // 2, width)] * 2,
        [
            pltpu.VMEM((part, 4 * tokens), BF16),
            pltpu.VMEM((4 * tokens, 3 * width), BF16),
            pltpu.VMEM((2, part // 2, 2 * width), F32),
            pltpu.VMEM((2, part // 2, width), F32),
            pltpu.SemaphoreType.DMA((20,)),
        ],
        far=3,
        after=(out_keep,),
        vmem=LATE_VMEM_BYTES,
    )
    pair_arrived = swap(pair_send, halved_bits[0])
    query_arrived = swap(query_send, halved_bits[1])

    def halve(arrays, next_bit, after, work=0):
        count, shape = len(arrays), (arrays[0].shape[0] // 2, arrays[0].shape[1])
        return call(
            functools.partial(halve_body, next_bit, count),
            "halve",
            arrays,
            [bf16(*shape)] * 2,
            [pltpu.VMEM((2, count, *shape), BF16), pltpu.SemaphoreType.DMA((2 * count,))],
            work=work,
            far=count,
            vmem=LATE_VMEM_BYTES,
            after=(after,),
        )

    def stepped(arrays, bits, after, work=0):
        send, keep = halve(arrays, bits[0], after, work)
        return [keep, swap(send, bits[0])], bits[1:], send

    out, out_left, last = stepped(
        [out_keep] + out_arrived, out_bits[2:] + [OUT_BIT], pair_send, LONG_WORK // 2
    )
    contrib_other = mirror(follows(contrib_mirror, last))
    returned_other = mirror(follows(returned_mirror, last))
    hidden_out = (
        hidden_in.astype(F32) + contrib.astype(F32) + contrib_other.astype(F32)
    ).astype(BF16)
    grad_in = (
        grad_out.astype(F32) + returned.astype(F32) + returned_other.astype(F32)
    ).astype(BF16)

    pair_total = pair_keep.astype(F32) + follows(pair_arrived, (last, query_arrived)).astype(F32)
    pair_total = pair_total.astype(BF16)
    pieces = exchange(pair_total, halved_bits[1:] + [col_bit])
    last = pair_total
    while out_left[1:]:
        out, out_left, last = stepped(out, out_left, last)
    query = [query_keep, query_arrived]
    for bit in halved_bits[2:]:
        query, _, last = stepped(query, [bit], last)
    rows, out_rows = features // replicas, half // replicas
    own, send_out, send_col, send_both, out_own = call(
        functools.partial(meet_body, col_bit),
        "meet",
        (*query, *out),
        [bf16(rows, width), bf16(rows + out_rows * (part // width), width)]
        + [bf16(rows, width)] * 2
        + [bf16(out_rows, part)],
        [
            pltpu.VMEM((2, 4 * rows, width), BF16),
            pltpu.VMEM((2, 2 * out_rows, part), BF16),
            pltpu.SemaphoreType.DMA((4,)),
        ],
        far=4,
        after=(last,),
        vmem=LATE_VMEM_BYTES,
    )
    blocks = [
        own,
        swap(send_out, OUT_BIT),
        swap(send_col, col_bit),
        swap(send_both, OUT_BIT, col_bit),
        out_own,
    ]
    grads = call(
        final_body,
        "final",
        (pieces.reshape(1 << len(halved_bits), -1, 2 * width), *blocks),
        [jax.ShapeDtypeStruct((rows, half), F32)] * 3
        + [jax.ShapeDtypeStruct((out_rows, features), F32)],
        vmem=LATE_VMEM_BYTES,
    )
    grad_value, grad_key, grad_query, grad_wout = (grad[None] for grad in grads)
    return (hidden_out, grad_in, grad_query, grad_key, grad_value, grad_wout)


def solution(mesh):
    in_specs = (
        P(("dp", "pipe"), None),
        P(("dp", "pipe"), None),
        P("pipe", None, None),
        P("pipe", None, None),
        P("pipe", None, None),
        P("pipe", None, None),
        P(),
    )
    out_specs = (
        P(("dp", "pipe"), None),
        P(("dp", "pipe"), None),
        P("pipe", "dp", None),
        P("pipe", "dp", None),
        P("pipe", "dp", None),
        P("pipe", "dp", None),
    )
    return jax.shard_map(
        on_device, mesh=mesh, in_specs=in_specs, out_specs=out_specs, check_vma=False
    )
```
